32 devices in a mesh: facet: 4 (over y, x), sub: 8 (over z, core).
Axes of the slice: x: 2, y: 2, z: 4, core: 2. Of those that a mesh axis runs over, the one named last changes fastest.
Arguments:
- facet_slab: bfloat16 [4, 2, 128, 8192], P('facet', None, 'sub'), may hold values from -6 to 6
- facet_offsets: int32 [4, 2], P('facet'), may hold values from 0 to 24576
- visibility_position: float32 [2, 32768], P(None, ('facet', 'sub')), may hold values from -32 to 32
- observed: float32 [2, 32768], P(None, ('facet', 'sub')), may hold values from -3 to 3
- visibility_subgrid: int32 [32768, 1], P(('facet', 'sub')), may hold values from 0 to 63; in each aligned block of 1024 rows (0 to 1023, 1024 to 2047, ...) at most 32 rows name the same one
- clip_levels: int32 [1024], P(('facet', 'sub')), may hold values from 1 to 8
Outputs:
- facet_adjoint: float32 [4, 2, 128, 8192], P('facet', None, 'sub')
- weighted_residual: float32 [2, 32768], P(None, ('facet', 'sub'))
The draws below stay inside these ranges and needn't reach their ends.
Inputs may be any that keep to these rules, and one draw needn't show every extreme that they name: `visibility_subgrid`: subgrid p * 8 + q covers subgrid row block p and column block q; within the rows of one device no subgrid is named more than 32 times. `facet_offsets`: column 0 is a facet's first image row, column 1 its first image column.
All inputs are finite; a program needn't handle non-finite values.
Results may differ from the reference program's by a relative error of at most 0.012.
Values may be sent and summed in bfloat16 or wider, within the bound.
A program may use at most 128 MiB of HBM per device.

```python
import math
import jax
import jax.numpy as jnp
import numpy as np
from jax import lax

FS = 8192
N_IMG = 32768
SUBG = 64
V_DEV = 1024
VIS_BLOCK = 32
FACETS = 4
ROWS = 128
NR = 8
NCOL = 8
NSG = 64
NVIS = 32768
MOST = 32
N_FACET = 4
N_SUB = 8


TWO_PI = 2.0 * math.pi


def tone_angles(count, frequency):
    position = jnp.arange(count, dtype=jnp.int32)
    phase_index = frequency[:, :, None] * position[None, None, :] % N_IMG
    return phase_index.astype(jnp.float32) * (TWO_PI / N_IMG)


def draw_facet_slab(key, part):
    keys = jax.random.split(jax.random.fold_in(key, 7301), 8)
    col_res = max(N_IMG // FS, 2)
    row_res = max(N_IMG // ROWS, 2)
    col_gap = jax.random.randint(keys[0], (FACETS, NCOL), col_res // 2 + 1, 2 * col_res + 1)
    col_side = jax.random.randint(keys[1], (FACETS, NCOL), 0, 2)
    col_base = jnp.arange(NCOL, dtype=jnp.int32)[None, :] * (N_IMG // NCOL)
    col_freq = (col_base + jnp.where(col_side == 1, SUBG - 1 + col_gap, N_IMG - col_gap)) % N_IMG
    row_gap = jax.random.randint(keys[2], (FACETS, NR), row_res // 2 + 1, 2 * row_res + 1)
    row_side = jax.random.randint(keys[3], (FACETS, NR), 0, 2)
    row_base = jnp.arange(NR, dtype=jnp.int32)[None, :] * (N_IMG // NR)
    row_freq = (row_base + jnp.where(row_side == 1, SUBG - 1 + row_gap, N_IMG - row_gap)) % N_IMG
    col_angle = tone_angles(FS, col_freq.astype(jnp.int32))
    row_angle = tone_angles(ROWS, row_freq.astype(jnp.int32))
    col_real = jnp.cos(col_angle)
    col_imag = jnp.sin(col_angle)
    row_real = jnp.cos(row_angle)
    row_imag = jnp.sin(row_angle)
    magnitude = jax.random.uniform(keys[4], (FACETS, NR, NCOL), jnp.float32, 0.06, 0.12)
    turn = jax.random.uniform(keys[5], (FACETS, NR, NCOL), jnp.float32, -math.pi, math.pi)
    amp_real = magnitude * jnp.cos(turn)
    amp_imag = magnitude * jnp.sin(turn)
    high = lax.Precision.HIGHEST
    mixed_real = jnp.einsum('fpr,fpq->frq', row_real, amp_real, precision=high) - jnp.einsum('fpr,fpq->frq', row_imag, amp_imag, precision=high)
    mixed_imag = jnp.einsum('fpr,fpq->frq', row_real, amp_imag, precision=high) + jnp.einsum('fpr,fpq->frq', row_imag, amp_real, precision=high)
    slab_real = jnp.einsum('frq,fqj->frj', mixed_real, col_real, precision=high) - jnp.einsum('frq,fqj->frj', mixed_imag, col_imag, precision=high)
    slab_imag = jnp.einsum('frq,fqj->frj', mixed_real, col_imag, precision=high) + jnp.einsum('frq,fqj->frj', mixed_imag, col_real, precision=high)
    noise = 0.15 * jax.random.normal(keys[6], (FACETS, 2, ROWS, FS), jnp.float32)
    slab = jnp.stack([slab_real, slab_imag], 1) + noise
    return jnp.clip(slab, -6.0, 6.0).astype(jnp.bfloat16)


def plant(values, rng, least, top_value):
    longest = values.shape.index(max(values.shape))
    spots = []
    for shift in (0, 1):
        where = [jax.random.randint(jax.random.fold_in(rng, axis), (), 0, length) for axis, length in enumerate(values.shape)]
        where[longest] = (where[longest] + shift) % values.shape[longest]
        spots.append(tuple(where))
    return values.at[spots[0]].set(least).at[spots[1]].set(top_value)


def level_of(own_key, extent, cuts, smallest, top_value):
    level, own = 1.0, jax.random.fold_in(own_key, 6)
    for dim, blocks in cuts:
        heights = jnp.exp(jax.random.uniform(jax.random.fold_in(own, dim), (blocks,), jnp.float32, smallest / len(cuts), top_value / len(cuts)))
        level = level * jnp.repeat(heights, extent[dim] // blocks).reshape([-1 if axis == dim else 1 for axis in range(len(extent))])
    return level


def shared_out(own_key, own, number, rows, number_of, top, bound, skew):
    ranking = jax.random.permutation(own_key, number_of)
    packed, common = portions_of(number_of, rows * top, bound, skew, True), portions_of(number_of, rows * top, bound, skew, False)
    places = jnp.arange(number_of)

    def named(tallies, turn):
        used = int((tallies > 0).sum())
        fixed = max(1, used // 4)
        passed = fixed + (places - fixed + turn * (used - fixed)) % max(1, number_of - fixed)
        return jnp.zeros((number_of,), jnp.int32).at[ranking[jnp.where(places < fixed, places, passed)]].set(jnp.asarray(tallies, jnp.int32))

    tallies = jnp.where(number % 4 == 0, named(packed, number // 4), named(common, number - number // 4 - 1))
    mixed = jax.random.permutation(jax.random.fold_in(own, 3), number_of)
    source_of, taker = mixed[0:number_of // 2 * 2:2], mixed[1:number_of // 2 * 2:2]
    margin = jnp.minimum(tallies[source_of] - 1, bound - tallies[taker]) // 2
    margin = jnp.where((source_of == ranking[0]) | (taker == ranking[0]) | (tallies[taker] == 0), 0, jnp.maximum(margin, 0))
    passed = jax.random.randint(jax.random.fold_in(own, 4), (number_of // 2,), 0, 1 << 20) % (margin + 1)
    tallies = tallies.at[source_of].add(-passed).at[taker].add(passed)
    members = jnp.searchsorted(jnp.cumsum(tallies), jnp.arange(rows * top), side="right").astype(jnp.int32)
    table = members.reshape(top, rows).T
    table = table[jax.random.permutation(jax.random.fold_in(own, 1), rows)]
    turn = jax.random.randint(jax.random.fold_in(own, 2), (rows, 1), 0, top)
    return jnp.take_along_axis(table, (jnp.arange(top)[None, :] + turn) % top, axis=1)


def portions_of(amount, total, reach, lean, full):
    loads = [(1 << 20) // math.isqrt(grade ** lean) + 1 for grade in range(1, amount + 1)]
    largest = reach if full else min(reach, max(-(-total // amount), total * loads[0] // sum(loads)))
    least = 1 if total - largest >= amount - 1 else 0
    holding, spare = [largest] + [least] * (amount - 1), total - largest - least * (amount - 1)
    while spare > 0:
        candidates = [i for i in range(1, amount) if holding[i] < largest] or [i for i in range(1, amount) if holding[i] < reach]
        pool, remaining = sum([loads[i] for i in candidates]), spare
        for i in candidates:
            more = min(reach - holding[i], max(1, remaining * loads[i] // pool), spare)
            holding[i] = holding[i] + more
            spare = spare - more
    return np.array(holding)


def normal_values(rng, shape, deviation, bound, cuts=(), kind=jnp.bfloat16):
    gain = level_of(rng, shape, cuts, -0.22, 0.18) if cuts else 1.0
    values = jax.random.normal(rng, shape, jnp.float32) * deviation * gain
    return jnp.minimum(jnp.maximum(values, -bound), bound).astype(kind)


def setup_inputs(seed: int = 0) -> dict:
    key_of = jax.random.split(jax.random.key(seed), 7)
    facet_slab = draw_facet_slab(jax.random.fold_in(key_of[6], 71), 0)
    facet_offsets = plant(jax.random.randint(key_of[1], (FACETS, 2), 0, N_IMG - FS + 1), jax.random.fold_in(key_of[1], 1), 0, N_IMG - FS).astype(jnp.int32)
    visibility_position = jnp.clip(jax.random.uniform(key_of[2], (2, NVIS), jnp.float32, -32.0, 32.0) * level_of(key_of[2], (2, NVIS), ((1, 32),), -0.4, 0.0), -32.0, 32.0)
    observed = normal_values(key_of[3], (2, NVIS), 0.5, 3.0, ((1, 32),), jnp.float32)
    visibility_subgrid_keys = jax.random.split(jax.random.fold_in(key_of[4], 1), NVIS // V_DEV)
    visibility_subgrid_turns = jax.random.permutation(jax.random.fold_in(key_of[4], 3), NVIS // V_DEV)
    visibility_subgrid = jax.vmap(lambda own, number: shared_out(jax.random.fold_in(key_of[4], 2), own, number, V_DEV, NSG, 1, MOST, 2))(visibility_subgrid_keys, visibility_subgrid_turns).reshape((NVIS, 1))
    clip_levels = plant(jax.random.randint(key_of[5], (NVIS // VIS_BLOCK,), 1, 9), jax.random.fold_in(key_of[5], 1), 1, 8).astype(jnp.int32)
    return {"facet_slab": facet_slab, "facet_offsets": facet_offsets, "visibility_position": visibility_position, "observed": observed, "visibility_subgrid": visibility_subgrid, "clip_levels": clip_levels}


TWO_PI = 2.0 * math.pi

def phase_pair(position, frequency, image_size, factor):
    phase_index = position[:, None] * frequency[None, :] % image_size
    angles = phase_index.astype(jnp.float32) * (-TWO_PI / image_size)
    return ((jnp.cos(angles) * factor).astype(jnp.bfloat16), (jnp.sin(angles) * factor).astype(jnp.bfloat16))

def column_tables(col_offset, facet_width, image_size, subgrid_size, column_count):
    position = col_offset + jnp.arange(facet_width, dtype=jnp.int32)
    fine_cos, fine_sin = phase_pair(position, jnp.arange(subgrid_size, dtype=jnp.int32), image_size, facet_width ** (-0.5))
    coarse_freq = jnp.arange(column_count, dtype=jnp.int32) * (image_size // column_count)
    coarse_cos, coarse_sin = phase_pair(position, coarse_freq, image_size, 1.0)
    return (fine_cos, fine_sin, coarse_cos, coarse_sin)

def row_tables(position, image_size, subgrid_size, row_blocks, total_rows):
    block_start = jnp.arange(row_blocks, dtype=jnp.int32)[:, None] * (image_size // row_blocks)
    frequency = (block_start + jnp.arange(subgrid_size, dtype=jnp.int32)[None, :]).reshape(-1)
    return phase_pair(position, frequency, image_size, 0.5 * total_rows ** (-0.5))

def column_forward(slab_real, slab_imag, tables):
    fine_cos, fine_sin, coarse_cos, coarse_sin = tables
    facet_width = fine_cos.shape[0]
    column_count = coarse_cos.shape[1]
    row_count = slab_real.shape[0]
    grouping = 4
    forward_matrix = jnp.concatenate([jnp.concatenate([fine_cos, fine_sin], 1), jnp.concatenate([-fine_sin, fine_cos], 1)], 0)
    real_wide = slab_real.astype(jnp.float32)[None]
    imag_wide = slab_imag.astype(jnp.float32)[None]

    def one_group(cos_sin):
        cos_group = cos_sin[0].astype(jnp.float32)[:, None, :]
        sin_group = cos_sin[1].astype(jnp.float32)[:, None, :]
        mod_real = (real_wide * cos_group - imag_wide * sin_group).astype(jnp.bfloat16)
        mod_imag = (real_wide * sin_group + imag_wide * cos_group).astype(jnp.bfloat16)
        joined = jnp.concatenate([mod_real, mod_imag], 2).reshape(grouping * row_count, 2 * facet_width)
        return jnp.dot(joined, forward_matrix, preferred_element_type=jnp.float32).reshape(grouping, row_count, -1)
    cos_groups = coarse_cos.T.reshape(column_count // grouping, grouping, facet_width)
    sin_groups = coarse_sin.T.reshape(column_count // grouping, grouping, facet_width)
    spectra = lax.map(one_group, (cos_groups, sin_groups))
    spectra = spectra.reshape(column_count, row_count, -1).transpose(1, 0, 2)
    return spectra.astype(jnp.bfloat16)

def row_forward(row_cos, row_sin, spectra):
    half_width = spectra.shape[2] // 2
    swapped = jnp.concatenate([-spectra[:, :, half_width:], spectra[:, :, :half_width]], 2)
    stacked = jnp.concatenate([spectra, swapped], 0)
    left_rows = jnp.concatenate([row_cos, row_sin], 0)
    flat = stacked.reshape(stacked.shape[0], -1)
    result = jnp.dot(left_rows.T, flat, preferred_element_type=jnp.float32)
    return result.reshape(left_rows.shape[1], spectra.shape[1], spectra.shape[2])

def row_adjoint(row_cos, row_sin, corrected_rows):
    half_width = corrected_rows.shape[2] // 2
    swapped = jnp.concatenate([corrected_rows[:, :, half_width:], -corrected_rows[:, :, :half_width]], 2)
    stacked = jnp.concatenate([corrected_rows, swapped], 0)
    left_rows = jnp.concatenate([row_cos, row_sin], 1)
    flat = stacked.reshape(stacked.shape[0], -1)
    result = jnp.dot(left_rows, flat, preferred_element_type=jnp.float32)
    return result.reshape(left_rows.shape[0], corrected_rows.shape[1], corrected_rows.shape[2])

def column_adjoint(images, tables):
    fine_cos, fine_sin, coarse_cos, coarse_sin = tables
    facet_width = fine_cos.shape[0]
    row_count = images.shape[0]
    column_count = images.shape[1]
    grouping = 4
    adjoint_matrix = jnp.concatenate([jnp.concatenate([fine_cos.T, -fine_sin.T], 1), jnp.concatenate([fine_sin.T, fine_cos.T], 1)], 0)
    image_groups = images.transpose(1, 0, 2).reshape(column_count // grouping, grouping * row_count, images.shape[2])
    cos_groups = coarse_cos.T.reshape(column_count // grouping, grouping, facet_width)
    sin_groups = coarse_sin.T.reshape(column_count // grouping, grouping, facet_width)

    def accumulate(running, inputs):
        image_group, cos_group, sin_group = inputs
        spread = jnp.dot(image_group, adjoint_matrix, preferred_element_type=jnp.float32).reshape(grouping, row_count, 2 * facet_width)
        spread_real = spread[:, :, :facet_width]
        spread_imag = spread[:, :, facet_width:]
        cos_wide = cos_group.astype(jnp.float32)[:, None, :]
        sin_wide = sin_group.astype(jnp.float32)[:, None, :]
        new_real = running[0] + lax.optimization_barrier(jnp.sum(cos_wide * spread_real + sin_wide * spread_imag, 0))
        new_imag = running[1] + lax.optimization_barrier(jnp.sum(cos_wide * spread_imag - sin_wide * spread_real, 0))
        return ((new_real, new_imag), None)
    initial = (jnp.zeros((row_count, facet_width), jnp.float32), jnp.zeros((row_count, facet_width), jnp.float32))
    finals, unused = lax.scan(accumulate, initial, (image_groups, cos_groups, sin_groups))
    return jnp.stack([finals[0], finals[1]])

def batched(pattern, left_operand, right_operand):
    return jnp.einsum(pattern, left_operand.astype(jnp.float32), right_operand.astype(jnp.float32))

def subgrid_pass(subgrids, payload, live_mask):
    subgrid_size = subgrids.shape[1]
    factor = subgrid_size ** (-0.5)
    offsets_grid = jnp.arange(subgrid_size, dtype=jnp.float32) * (TWO_PI / subgrid_size)
    angle_left = payload[0][:, :, None] * offsets_grid
    angle_right = payload[1][:, :, None] * offsets_grid
    left_real = jnp.cos(angle_left) * factor
    left_imag = jnp.sin(angle_left) * factor
    right_real = (jnp.cos(angle_right) * factor).astype(jnp.bfloat16)
    right_imag = (jnp.sin(angle_right) * factor).astype(jnp.bfloat16)
    first_basis = jnp.concatenate([right_real, -right_imag], 2)
    second_basis = jnp.concatenate([right_imag, right_real], 2)
    inner_real = batched('ksc,knc->kns', subgrids, first_basis)
    inner_imag = batched('ksc,knc->kns', subgrids, second_basis)
    predicted_real = lax.optimization_barrier(jnp.sum(left_real * inner_real - left_imag * inner_imag, 2))
    predicted_imag = lax.optimization_barrier(jnp.sum(left_real * inner_imag + left_imag * inner_real, 2))
    misfit_real = payload[2] - predicted_real
    misfit_imag = payload[3] - predicted_imag
    threshold = payload[4] + (1.0 - live_mask)
    magnitude = jnp.sqrt(misfit_real * misfit_real + misfit_imag * misfit_imag)
    weight = live_mask * threshold / jnp.maximum(magnitude, threshold)
    weighted_real = weight * misfit_real
    weighted_imag = weight * misfit_imag
    phasor_real = (left_real * weighted_real[:, :, None] + left_imag * weighted_imag[:, :, None]).astype(jnp.bfloat16)
    phasor_imag = (left_real * weighted_imag[:, :, None] - left_imag * weighted_real[:, :, None]).astype(jnp.bfloat16)
    gridded = batched('kms,kmc->ksc', jnp.concatenate([phasor_real, phasor_imag], 1), jnp.concatenate([first_basis, second_basis], 1))
    return (gridded.astype(jnp.bfloat16), weighted_real, weighted_imag)

def reference(facet_slab, facet_offsets, visibility_position, observed, visibility_subgrid, clip_levels):
    visibility_count = visibility_position.shape[1]
    total_rows = facet_slab.shape[2]
    kept_tables = []
    kept_rows = []
    summed = None
    for facet_index in range(FACETS):
        tables = column_tables(facet_offsets[facet_index, 1], FS, N_IMG, SUBG, NCOL)
        spectra = column_forward(facet_slab[facet_index, 0], facet_slab[facet_index, 1], tables)
        row_position = facet_offsets[facet_index, 0] + jnp.arange(total_rows, dtype=jnp.int32)
        row_cos, row_sin = row_tables(row_position, N_IMG, SUBG, NR, total_rows)
        contribution = row_forward(row_cos, row_sin, spectra)
        summed = contribution if summed is None else summed + contribution
        kept_tables.append(tables)
        kept_rows.append((row_cos, row_sin))
    subgrids = summed.reshape(NR, SUBG, NCOL, 2 * SUBG).transpose(0, 2, 1, 3).reshape(NSG, SUBG, 2 * SUBG).astype(jnp.bfloat16)
    identity = visibility_subgrid[:, 0]
    sort_order = jnp.argsort(identity, stable=True).astype(jnp.int32)
    sorted_ids = identity[sort_order]
    first_seen = jnp.searchsorted(sorted_ids, sorted_ids, side='left').astype(jnp.int32)
    ranked = jnp.arange(visibility_count, dtype=jnp.int32) - first_seen
    capacity = N_FACET * N_SUB * MOST
    slot_table = jnp.full((NSG, capacity), visibility_count, jnp.int32).at[sorted_ids, ranked].set(sort_order)
    levels = jnp.repeat(clip_levels, VIS_BLOCK).astype(jnp.float32) * 0.25
    rows_all = jnp.stack([visibility_position[0], visibility_position[1], observed[0], observed[1], levels])
    rows_all = jnp.concatenate([rows_all, jnp.zeros((5, 1), jnp.float32)], 1)
    live_all = jnp.concatenate([jnp.ones((visibility_count,), jnp.float32), jnp.zeros((1,), jnp.float32)])

    def per_subgrid(element):
        index_row, subgrid = element
        payload = rows_all[:, index_row][:, None, :]
        live_mask = live_all[index_row][None, :]
        gridded, weighted_real, weighted_imag = subgrid_pass(subgrid[None], payload, live_mask)
        return (gridded[0], weighted_real[0], weighted_imag[0])
    corrected, result_real, result_imag = lax.map(per_subgrid, (slot_table, subgrids))
    weighted = jnp.zeros((2, visibility_count + 1), jnp.float32)
    weighted = weighted.at[0, slot_table].set(result_real).at[1, slot_table].set(result_imag)
    weighted_residual = weighted[:, :visibility_count]
    corrected_rows = corrected.reshape(NR, NCOL, SUBG, 2 * SUBG).transpose(0, 2, 1, 3).reshape(NR * SUBG, NCOL, 2 * SUBG)
    adjoints = []
    for facet_index in range(FACETS):
        row_cos, row_sin = kept_rows[facet_index]
        images = row_adjoint(row_cos, row_sin, corrected_rows).astype(jnp.bfloat16)
        adjoints.append(column_adjoint(images, kept_tables[facet_index]))
    return (jnp.stack(adjoints), weighted_residual)
```

```python
import functools
import math

import jax
import jax.numpy as jnp
from jax import lax
from jax.experimental import pallas as pl
from jax.experimental.pallas import tpu as pltpu
from jax.sharding import PartitionSpec as P

N_IMG = 32768
SUBG = 64
PR_DEV = 2
VIS_BLOCK = 32
LANES = 128
CHUNK = 512

TWO_PI = 2.0 * math.pi
MESH = pl.DeviceIdType.MESH
F32 = jnp.float32
BF16 = jnp.bfloat16


def cos_sin(turns):
    quarter = jnp.floor(turns * 4.0 + 0.5)
    y = (turns - quarter * 0.25) * TWO_PI
    y2 = y * y
    s = y * (1.0 + y2 * (-1 / 6 + y2 * (1 / 120 + y2 * (-1 / 5040 + y2 * (1 / 362880)))))
    c = 1.0 + y2 * (-0.5 + y2 * (1 / 24 + y2 * (-1 / 720 + y2 * (1 / 40320))))
    k = quarter.astype(jnp.int32)
    odd = (k & 1) == 1
    cos = jnp.where(odd, s, c)
    sin = jnp.where(odd, c, s)
    cos = jnp.where(((k + 1) & 2) == 2, -cos, cos)
    sin = jnp.where((k & 2) == 2, -sin, sin)
    return cos, sin


def table(index):
    return cos_sin((index & (N_IMG - 1)).astype(F32) * (-1.0 / N_IMG))


def iota(shape, dim):
    return lax.broadcasted_iota(jnp.int32, shape, dim)


def dot(a, b):
    return jnp.dot(a, b, preferred_element_type=F32)


def dot_nt(a, b):
    return lax.dot_general(a, b, (((1,), (1,)), ((), ())), preferred_element_type=F32)


def dot_tn(a, b):
    return lax.dot_general(a, b, (((0,), (0,)), ((), ())), preferred_element_type=F32)


def three_parts(x):
    high = x.astype(BF16)
    rest = x - high.astype(F32)
    middle = rest.astype(BF16)
    low = (rest - middle.astype(F32)).astype(BF16)
    return high, middle, low


def kernel(
    facet_count,
    sub_count,
    offsets_ref,
    slab_ref,
    position_ref,
    observed_ref,
    subgrid_ref,
    clip_ref,
    adjoint_ref,
    residual_ref,
    vis_send,
    vis_recv,
    spec_send,
    spec_recv,
    back_send,
    back_recv,
    image_send,
    image_recv,
    place_ref,
    owner_ref,
    fine_one,
    fine_two,
    step_cos,
    step_sin,
    acc_ref,
    row_cos,
    row_sin,
    left_real,
    left_imag,
    basis_one,
    basis_two,
    known,
    corrected,
    send_sems,
    recv_sems,
):
    devices = facet_count * sub_count
    my_facet = lax.axis_index("facet")
    my_sub = lax.axis_index("sub")
    me = my_facet * sub_count + my_sub
    columns = sub_count
    rows = slab_ref.shape[2]
    width = slab_ref.shape[3]
    vis = position_ref.shape[1]
    row_blocks = PR_DEV * facet_count
    most = max(2, 2 * vis // (row_blocks * columns))
    span = PR_DEV * most
    group = LANES // span
    slots = devices * span
    total_rows = rows * sub_count
    tile = (8, LANES)

    def partner(i):
        other = lax.rem(me + i, devices)
        return other, (lax.div(other, sub_count), lax.rem(other, sub_count))

    barrier = pltpu.get_barrier_semaphore()

    @pl.loop(1, devices)
    def greet(i):
        unused, where = partner(i)
        pl.semaphore_signal(barrier, inc=1, device_id=where, device_id_type=MESH)

    def send_all(kind, source_of, target):
        @pl.loop(1, devices)
        def one(i):
            other, where = partner(i)
            pltpu.make_async_remote_copy(
                src_ref=source_of(other),
                dst_ref=target.at[me],
                send_sem=send_sems.at[kind],
                recv_sem=recv_sems.at[kind],
                device_id=where,
                device_id_type=MESH,
            ).start()

    def wait_all(sems, kind, target):
        whole = target.at[pl.ds(0, devices - 1)]
        pltpu.make_async_copy(whole, whole, sems.at[kind]).wait()

    ids = subgrid_ref[...].astype(F32)
    block_row = jnp.floor((ids + 0.5) * (1.0 / columns))
    block_col = ids - block_row * columns
    pair = jnp.floor((block_row + 0.5) * (1.0 / PR_DEV))
    local = block_row - pair * PR_DEV
    owner = pair * sub_count + block_col
    key = owner * PR_DEV + local
    key_rows = iota((devices * PR_DEV, vis), 0).astype(F32)
    same = jnp.where(key_rows == key, 1.0, 0.0)
    earlier = jnp.where(iota((vis, vis), 0) < iota((vis, vis), 1), 1.0, 0.0).astype(BF16)
    counts = dot(same.astype(BF16), earlier)
    rank = jnp.sum(same * counts, 0, keepdims=True)
    my_place = lax.rem(me, group) * span
    slot = my_place.astype(F32) + local * most + rank
    place = jnp.where(iota((LANES, vis), 0).astype(F32) == slot, 1.0, 0.0).astype(BF16)
    place_ref[...] = place
    owner_ref[...] = owner
    clip = jnp.broadcast_to(clip_ref[...].astype(F32), (8, clip_ref.shape[1]))
    block_start = iota((clip_ref.shape[1], vis), 0) * VIS_BLOCK
    block_at = iota((clip_ref.shape[1], vis), 1)
    in_block = (block_at >= block_start) & (block_at < block_start + VIS_BLOCK)
    spread_out = jnp.where(in_block, 1.0, 0.0).astype(BF16)
    levels = dot(clip.astype(BF16), spread_out)[0:1] * 0.25
    values = jnp.concatenate(
        [position_ref[...], observed_ref[...], levels, jnp.zeros((3, vis), F32)], 0
    )
    chosen = iota((devices, 8, vis), 0).astype(F32) == owner[None]
    packed = jnp.zeros((devices * 8, LANES), F32)
    for part in three_parts(values):
        masked = jnp.where(chosen, part.astype(F32)[None], 0.0)
        masked = masked.reshape(devices * 8, vis).astype(BF16)
        packed = packed + dot_nt(masked, place)
    row_offset = offsets_ref[0, 0].astype(F32)
    packed = packed.reshape(devices, 8, LANES)
    packed = jnp.where(iota((devices, 8, LANES), 1) == 5, row_offset, packed)
    vis_send[...] = packed
    vis_recv[me] = vis_send[me]

    pl.semaphore_wait(barrier, devices - 1)
    send_all(0, lambda other: vis_send.at[other], vis_recv)

    col_offset = offsets_ref[0, 1]
    lane = iota((LANES, LANES), 1)
    tone = lane & (SUBG - 1)
    first_half = lane < SUBG
    base_cos, base_sin = table((col_offset + iota((LANES, LANES), 0)) * tone)
    scale = width ** (-0.5)
    base_one = jnp.where(first_half, base_cos, base_sin) * scale
    base_two = jnp.where(first_half, -base_sin, base_cos) * scale
    step_count = width // LANES
    step_tone = iota((step_count, LANES), 1) & (SUBG - 1)
    sc, ss = table(iota((step_count, LANES), 0) * LANES * step_tone)
    step_cos[...] = sc
    step_sin[...] = ss
    coarse_step = N_IMG // columns
    coarse_at = col_offset + iota((columns, LANES), 1)
    coarse_index = ((coarse_at & (columns - 1)) * iota((columns, LANES), 0)) * coarse_step
    coarse_cos, coarse_sin = table(coarse_index)
    coarse_cos = coarse_cos.astype(BF16).astype(F32)
    coarse_sin = coarse_sin.astype(BF16).astype(F32)
    copies = CHUNK // LANES
    wide_cos = jnp.concatenate([coarse_cos] * copies, 1)
    wide_sin = jnp.concatenate([coarse_sin] * copies, 1)
    acc_ref[...] = jnp.zeros_like(acc_ref)

    @pl.loop(0, width // CHUNK)
    def forward(c):
        at = pl.multiple_of(c * CHUNK, CHUNK)
        ones, twos = [], []
        for k in range(copies):
            ca = step_cos[pl.ds(c * copies + k, 1), :]
            sa = step_sin[pl.ds(c * copies + k, 1), :]
            ones.append((ca * base_one + sa * base_two).astype(BF16))
            twos.append((ca * base_two - sa * base_one).astype(BF16))
        one = jnp.concatenate(ones, 0)
        two = jnp.concatenate(twos, 0)
        fine_one[pl.ds(at, CHUNK), :] = one
        fine_two[pl.ds(at, CHUNK), :] = two
        real = slab_ref[0, 0, :, pl.ds(at, CHUNK)].astype(F32)
        imag = slab_ref[0, 1, :, pl.ds(at, CHUNK)].astype(F32)
        mod_real, mod_imag = [], []
        for q in range(columns):
            cc = wide_cos[q : q + 1]
            cs = wide_sin[q : q + 1]
            mod_real.append((real * cc - imag * cs).astype(BF16))
            mod_imag.append((real * cs + imag * cc).astype(BF16))
        acc_ref[...] += dot(jnp.concatenate(mod_real, 0), one) + dot(
            jnp.concatenate(mod_imag, 0), two
        )

    spec_send[...] = acc_ref[...].astype(BF16).reshape(columns, rows, LANES)
    spec_recv[me] = spec_send[my_sub]
    send_all(1, lambda other: spec_send.at[lax.rem(other, sub_count)], spec_recv)

    wait_all(recv_sems, 0, vis_recv)
    table_lane = iota((total_rows, LANES), 1)
    table_block = PR_DEV * my_facet + (table_lane >= SUBG).astype(jnp.int32)
    row_tone = table_block * (N_IMG // row_blocks) + (table_lane & (SUBG - 1))
    row_scale = 0.5 * total_rows ** (-0.5)
    for f in range(facet_count):
        start = vis_recv[f * sub_count][5:6, :].astype(jnp.int32)
        rc, rs = table((start + iota((total_rows, LANES), 0)) * row_tone)
        row_cos[pl.ds(f * total_rows, total_rows), :] = (rc * row_scale).astype(BF16)
        row_sin[pl.ds(f * total_rows, total_rows), :] = (rs * row_scale).astype(BF16)
    for j in range(slots // LANES):
        merged = vis_recv[j * group]
        for i in range(1, group):
            merged = merged + vis_recv[j * group + i]
        known[:, j * LANES : (j + 1) * LANES] = merged

    factor = SUBG ** (-0.5)

    @pl.loop(0, slots // CHUNK)
    def bases(c):
        at = pl.ds(pl.multiple_of(c * CHUNK, CHUNK), CHUNK)
        grid = iota((SUBG, CHUNK), 0).astype(F32) * (1.0 / SUBG)
        lr, li = cos_sin(known[0:1, at] * grid)
        left_real[:, at] = lr * factor
        left_imag[:, at] = li * factor
        rr, ri = cos_sin(known[1:2, at] * grid)
        rr = rr * factor
        ri = ri * factor
        basis_one[:, at] = jnp.concatenate([rr, -ri], 0).astype(BF16)
        basis_two[:, at] = jnp.concatenate([ri, rr], 0).astype(BF16)

    wait_all(recv_sems, 1, spec_recv)
    spectra = spec_recv[...].reshape(facet_count * total_rows, LANES).astype(F32)
    half = iota((1, LANES), 1) < SUBG
    turned = pltpu.roll(spectra, SUBG, 1)
    turned = jnp.where(half, -turned, turned)
    subgrids = dot_tn(row_cos[...], spectra.astype(BF16)) + dot_tn(
        row_sin[...], turned.astype(BF16)
    )
    subgrids = subgrids.astype(BF16)
    acc_out = jnp.zeros((LANES, LANES), F32)
    for c in range(slots // CHUNK):
        at = slice(c * CHUNK, (c + 1) * CHUNK)
        lr = left_real[:, at]
        li = left_imag[:, at]
        one = basis_one[:, at]
        two = basis_two[:, at]
        slot_lane = iota((1, CHUNK), 1) & (span - 1)
        second = slot_lane >= most
        inner_real = dot(subgrids, one)
        inner_imag = dot(subgrids, two)
        inner_real = jnp.where(second, inner_real[SUBG:], inner_real[:SUBG])
        inner_imag = jnp.where(second, inner_imag[SUBG:], inner_imag[:SUBG])
        level = known[4:5, at]
        live = jnp.where(level > 0.0, 1.0, 0.0)
        misfit_real = known[2:3, at] - jnp.sum(lr * inner_real - li * inner_imag, 0, keepdims=True)
        misfit_imag = known[3:4, at] - jnp.sum(lr * inner_imag + li * inner_real, 0, keepdims=True)
        threshold = level + (1.0 - live)
        magnitude = jnp.sqrt(misfit_real * misfit_real + misfit_imag * misfit_imag)
        weight = live * threshold / jnp.maximum(magnitude, threshold)
        wr = weight * misfit_real
        wi = weight * misfit_imag
        blank = jnp.zeros((6, LANES), F32)
        for k in range(copies):
            part = slice(k * LANES, (k + 1) * LANES)
            back_send[c * copies + k] = jnp.concatenate([wr[:, part], wi[:, part], blank], 0)
        pr = lr * wr + li * wi
        pi = lr * wi - li * wr
        pr = jnp.concatenate([jnp.where(second, 0.0, pr), jnp.where(second, pr, 0.0)], 0)
        pi = jnp.concatenate([jnp.where(second, 0.0, pi), jnp.where(second, pi, 0.0)], 0)
        acc_out = acc_out + dot_nt(pr.astype(BF16), one) + dot_nt(pi.astype(BF16), two)
    back_recv[me] = back_send[lax.div(me, group)]
    send_all(2, lambda other: back_send.at[lax.div(other, group)], back_recv)

    corrected[...] = acc_out.astype(BF16)
    gridded = corrected[...].astype(F32)
    turned = pltpu.roll(gridded, SUBG, 1)
    turned = jnp.where(half, turned, -turned)
    parts = dot(row_cos[...], gridded.astype(BF16)) + dot(row_sin[...], turned.astype(BF16))
    image_send[...] = parts.astype(BF16).reshape(devices, rows, LANES)
    image_recv[me] = image_send[me]
    send_all(3, lambda other: image_send.at[other], image_recv)

    wait_all(recv_sems, 2, back_recv)
    returned = back_recv[...].reshape(devices * 8, LANES)
    found = jnp.zeros((devices * 8, vis), F32)
    for part in three_parts(returned):
        found = found + dot(part, place_ref[...])
    chosen = iota((devices, 8, vis), 0).astype(F32) == owner_ref[...][None]
    found = jnp.sum(jnp.where(chosen, found.reshape(devices, 8, vis), 0.0), 0)
    residual_ref[...] = found[0:2]

    wait_all(recv_sems, 3, image_recv)
    held = image_recv[...].astype(F32).reshape(facet_count, columns * rows, LANES)
    images = held[0]
    for f in range(1, facet_count):
        images = images + held[f]
    images = images.astype(BF16)

    @pl.loop(0, width // CHUNK)
    def adjoint(c):
        at = pl.ds(pl.multiple_of(c * CHUNK, CHUNK), CHUNK)
        real = dot_nt(images, fine_one[at, :])
        imag = dot_nt(images, fine_two[at, :])
        out_real = jnp.zeros((rows, CHUNK), F32)
        out_imag = jnp.zeros((rows, CHUNK), F32)
        for q in range(columns):
            cc = wide_cos[q : q + 1]
            cs = wide_sin[q : q + 1]
            sr = real[q * rows : (q + 1) * rows]
            si = imag[q * rows : (q + 1) * rows]
            out_real = out_real + (cc * sr + cs * si)
            out_imag = out_imag + (cc * si - cs * sr)
        adjoint_ref[0, 0, :, at] = out_real
        adjoint_ref[0, 1, :, at] = out_imag

    wait_all(send_sems, 0, vis_recv)
    wait_all(send_sems, 1, spec_recv)
    wait_all(send_sems, 2, back_recv)
    wait_all(send_sems, 3, image_recv)


def on_device(
    facet_slab, facet_offsets, visibility_position, observed, visibility_subgrid, clip_levels
):
    sub_count = lax.axis_size("sub")
    facet_count = lax.axis_size("facet")
    devices = sub_count * facet_count
    rows = facet_slab.shape[2]
    width = facet_slab.shape[3]
    vis = visibility_position.shape[1]
    most = max(2, 2 * vis // (PR_DEV * facet_count * sub_count))
    slots = devices * PR_DEV * most
    all_rows = devices * rows
    vmem = pl.BlockSpec(memory_space=pltpu.VMEM)
    smem = pl.BlockSpec(memory_space=pltpu.SMEM)
    return pl.pallas_call(
        functools.partial(kernel, facet_count, sub_count),
        out_shape=(
            jax.ShapeDtypeStruct(facet_slab.shape, F32),
            jax.ShapeDtypeStruct((2, vis), F32),
        ),
        in_specs=[smem] + [vmem] * 5,
        out_specs=(vmem, vmem),
        scratch_shapes=[
            pltpu.VMEM((devices, 8, LANES), F32),
            pltpu.VMEM((devices, 8, LANES), F32),
            pltpu.VMEM((sub_count, rows, LANES), BF16),
            pltpu.VMEM((devices, rows, LANES), BF16),
            pltpu.VMEM((slots // LANES, 8, LANES), F32),
            pltpu.VMEM((devices, 8, LANES), F32),
            pltpu.VMEM((devices, rows, LANES), BF16),
            pltpu.VMEM((devices, rows, LANES), BF16),
            pltpu.VMEM((LANES, vis), BF16),
            pltpu.VMEM((1, vis), F32),
            pltpu.VMEM((width, LANES), BF16),
            pltpu.VMEM((width, LANES), BF16),
            pltpu.VMEM((width // LANES, LANES), F32),
            pltpu.VMEM((width // LANES, LANES), F32),
            pltpu.VMEM((sub_count * rows, LANES), F32),
            pltpu.VMEM((all_rows, LANES), BF16),
            pltpu.VMEM((all_rows, LANES), BF16),
            pltpu.VMEM((SUBG, slots), F32),
            pltpu.VMEM((SUBG, slots), F32),
            pltpu.VMEM((2 * SUBG, slots), BF16),
            pltpu.VMEM((2 * SUBG, slots), BF16),
            pltpu.VMEM((8, slots), F32),
            pltpu.VMEM((LANES, LANES), BF16),
            pltpu.SemaphoreType.DMA((4,)),
            pltpu.SemaphoreType.DMA((4,)),
        ],
        compiler_params=pltpu.CompilerParams(
            collective_id=0, has_side_effects=True, vmem_limit_bytes=56 * 1024 * 1024
        ),
    )(
        facet_offsets,
        facet_slab,
        visibility_position,
        observed,
        visibility_subgrid.reshape(1, vis),
        clip_levels.reshape(1, -1),
    )


def solution(mesh):
    placed = (
        P("facet", None, "sub", None),
        P("facet", None),
        P(None, ("facet", "sub")),
        P(None, ("facet", "sub")),
        P(("facet", "sub"), None),
        P(("facet", "sub")),
    )
    return jax.shard_map(
        on_device,
        mesh=mesh,
        in_specs=placed,
        out_specs=(P("facet", None, "sub", None), P(None, ("facet", "sub"))),
        check_vma=False,
    )
```

```python
import functools
import math

import jax
import jax.numpy as jnp
from jax import lax
from jax.experimental import pallas as pl
from jax.experimental.pallas import tpu as pltpu
from jax.sharding import PartitionSpec as P

N_IMG = 32768
SUBG = 64
PR_DEV = 2
VIS_BLOCK = 32
LANES = 128
CHUNK = 512

TWO_PI = 2.0 * math.pi
MESH = pl.DeviceIdType.MESH
F32 = jnp.float32
BF16 = jnp.bfloat16


def cos_sin(turns):
    quarter = jnp.floor(turns * 4.0 + 0.5)
    y = (turns - quarter * 0.25) * TWO_PI
    y2 = y * y
    s = y * (1.0 + y2 * (-1 / 6 + y2 * (1 / 120 + y2 * (-1 / 5040 + y2 * (1 / 362880)))))
    c = 1.0 + y2 * (-0.5 + y2 * (1 / 24 + y2 * (-1 / 720 + y2 * (1 / 40320))))
    k = quarter.astype(jnp.int32)
    odd = (k & 1) == 1
    cos = jnp.where(odd, s, c)
    sin = jnp.where(odd, c, s)
    cos = jnp.where(((k + 1) & 2) == 2, -cos, cos)
    sin = jnp.where((k & 2) == 2, -sin, sin)
    return cos, sin


def table(index):
    return cos_sin((index & (N_IMG - 1)).astype(F32) * (-1.0 / N_IMG))


def iota(shape, dim):
    return lax.broadcasted_iota(jnp.int32, shape, dim)


def dot(a, b):
    return jnp.dot(a, b, preferred_element_type=F32)


def dot_nt(a, b):
    return lax.dot_general(a, b, (((1,), (1,)), ((), ())), preferred_element_type=F32)


def dot_tn(a, b):
    return lax.dot_general(a, b, (((0,), (0,)), ((), ())), preferred_element_type=F32)


def three_parts(x):
    high = x.astype(BF16)
    rest = x - high.astype(F32)
    middle = rest.astype(BF16)
    low = (rest - middle.astype(F32)).astype(BF16)
    return high, middle, low


def column_tables(col_offset, columns, width, matrix_ref, step_cos, step_sin):
    lane = iota((LANES, LANES), 1)
    first_half = lane < SUBG
    base_cos, base_sin = table((col_offset + iota((LANES, LANES), 0)) * (lane & (SUBG - 1)))
    scale = width ** (-0.5)
    base_one = jnp.where(first_half, base_cos, base_sin) * scale
    base_two = jnp.where(first_half, -base_sin, base_cos) * scale
    coarse_step = N_IMG // columns
    residue = (col_offset + iota((columns, LANES), 0)) & (columns - 1)
    for q in range(columns):
        cc, cs = table(residue * (q * coarse_step))
        cc = jnp.concatenate([cc] * (LANES // columns), 0)
        cs = jnp.concatenate([cs] * (LANES // columns), 0)
        at = slice(q * LANES, (q + 1) * LANES)
        matrix_ref[:LANES, at] = (cc * base_one + cs * base_two).astype(BF16)
        matrix_ref[LANES:, at] = (cc * base_two - cs * base_one).astype(BF16)
    steps = width // LANES
    step_lane = iota((steps, LANES), 1)
    sc, ss = table(iota((steps, LANES), 0) * LANES * (step_lane & (SUBG - 1)))
    step_cos[...] = sc
    step_sin[...] = jnp.where(step_lane < SUBG, ss, -ss)


def kernel(
    facet_count,
    sub_count,
    offsets_ref,
    slab_ref,
    position_ref,
    observed_ref,
    subgrid_ref,
    clip_ref,
    image_ref,
    residual_ref,
    vis_send,
    vis_recv,
    spec_send,
    spec_recv,
    back_send,
    back_recv,
    image_send,
    image_recv,
    place_ref,
    owner_ref,
    slab_rows,
    matrix,
    step_cos,
    step_sin,
    row_wide,
    row_tall,
    left_real,
    left_imag,
    basis_one,
    basis_two,
    known,
    send_sems,
    recv_sems,
):
    devices = facet_count * sub_count
    my_facet = lax.axis_index("facet")
    my_sub = lax.axis_index("sub")
    me = my_facet * sub_count + my_sub
    columns = sub_count
    rows = slab_ref.shape[2]
    width = slab_ref.shape[3]
    vis = position_ref.shape[1]
    row_blocks = PR_DEV * facet_count
    most = max(2, 2 * vis // (row_blocks * columns))
    span = PR_DEV * most
    group = LANES // span
    slots = devices * span
    total_rows = rows * sub_count

    partners = []
    for df in range(facet_count):
        facet = my_facet + df
        facet = jnp.where(facet >= facet_count, facet - facet_count, facet)
        for ds in range(sub_count):
            sub = my_sub + ds
            sub = jnp.where(sub >= sub_count, sub - sub_count, sub)
            if df or ds:
                partners.append((facet, sub))

    barrier = pltpu.get_barrier_semaphore()
    for where in partners:
        pl.semaphore_signal(barrier, inc=1, device_id=where, device_id_type=MESH)

    def send_all(kind, source_of, target):
        for facet, sub in partners:
            pltpu.make_async_remote_copy(
                src_ref=source_of(facet, sub),
                dst_ref=target.at[me],
                send_sem=send_sems.at[kind],
                recv_sem=recv_sems.at[kind],
                device_id=(facet, sub),
                device_id_type=MESH,
            ).start()

    def wait_all(sems, kind, target):
        whole = target.at[pl.ds(0, devices - 1)]
        pltpu.make_async_copy(whole, whole, sems.at[kind]).wait()

    ids = subgrid_ref[...].astype(F32)
    block_row = jnp.floor((ids + 0.5) * (1.0 / columns))
    block_col = ids - block_row * columns
    pair = jnp.floor((block_row + 0.5) * (1.0 / PR_DEV))
    local = block_row - pair * PR_DEV
    owner = pair * sub_count + block_col
    key = owner * PR_DEV + local
    key_rows = iota((devices * PR_DEV, vis), 0).astype(F32)
    same = jnp.where(key_rows == key, 1.0, 0.0)
    earlier = jnp.where(iota((LANES, LANES), 0) < iota((LANES, LANES), 1), 1.0, 0.0).astype(BF16)
    before = jnp.zeros((devices * PR_DEV, 1), F32)
    ranks = []
    for k in range(vis // LANES):
        block = same[:, k * LANES : (k + 1) * LANES]
        counts = dot(block.astype(BF16), earlier) + before
        ranks.append(jnp.sum(block * counts, 0, keepdims=True))
        before = before + jnp.sum(block, 1, keepdims=True)
    rank = jnp.concatenate(ranks, 1)
    my_place = lax.rem(me, group) * span
    slot = my_place.astype(F32) + local * most + rank
    place = jnp.where(iota((LANES, vis), 0).astype(F32) == slot, 1.0, 0.0).astype(BF16)
    place_ref[...] = place
    owner_ref[...] = owner
    clip = jnp.broadcast_to(clip_ref[...].astype(F32), (8, clip_ref.shape[1]))
    block_start = iota((clip_ref.shape[1], vis), 0) * VIS_BLOCK
    block_at = iota((clip_ref.shape[1], vis), 1)
    in_block = (block_at >= block_start) & (block_at < block_start + VIS_BLOCK)
    spread_out = jnp.where(in_block, 1.0, 0.0).astype(BF16)
    levels = dot(clip.astype(BF16), spread_out)[0:1] * 0.25
    values = jnp.concatenate(
        [position_ref[...], observed_ref[...], levels, jnp.zeros((3, vis), F32)], 0
    )
    chosen = iota((devices, 8, vis), 0).astype(F32) == owner[None]
    packed = jnp.zeros((devices * 8, LANES), F32)
    for part in three_parts(values):
        masked = jnp.where(chosen, part.astype(F32)[None], 0.0)
        masked = masked.reshape(devices * 8, vis).astype(BF16)
        packed = packed + dot_nt(masked, place)
    row_offset = offsets_ref[0, 0].astype(F32)
    packed = packed.reshape(devices, 8, LANES)
    packed = jnp.where(iota((devices, 8, LANES), 1) == 5, row_offset, packed)
    vis_send[...] = packed
    vis_recv[me] = vis_send[me]

    pl.semaphore_wait(barrier, devices - 1)
    send_all(0, lambda f, s: vis_send.at[f * sub_count + s], vis_recv)

    column_tables(offsets_ref[0, 1], columns, width, matrix, step_cos, step_sin)
    steps = width // LANES
    for h in range(steps):
        part = slice(h * LANES, (h + 1) * LANES)
        for c in range(2):
            slab_rows[h * rows : (h + 1) * rows, c * LANES : (c + 1) * LANES] = slab_ref[
                0, c, :, part
            ]
    taken = 16
    for q in range(0, columns, 2):
        both = matrix[:, q * LANES : (q + 2) * LANES]
        straight = jnp.zeros((rows, 2 * LANES), F32)
        crossed = jnp.zeros((rows, 2 * LANES), F32)
        for h in range(0, steps, taken):
            spread = dot(slab_rows[h * rows : (h + taken) * rows, :], both)
            for k in range(taken):
                piece = spread[k * rows : (k + 1) * rows]
                sc = step_cos[h + k : h + k + 1, :]
                ss = step_sin[h + k : h + k + 1, :]
                straight = straight + piece * jnp.concatenate([sc, sc], 1)
                crossed = crossed + piece * jnp.concatenate([ss, ss], 1)
        for k in range(2):
            part = slice(k * LANES, (k + 1) * LANES)
            spectrum = straight[:, part] + pltpu.roll(crossed[:, part], SUBG, 1)
            spec_send[q + k] = spectrum.astype(BF16)

    spec_recv[me] = spec_send[my_sub]
    send_all(1, lambda f, s: spec_send.at[s], spec_recv)

    wait_all(recv_sems, 0, vis_recv)
    table_lane = iota((total_rows, LANES), 1)
    table_block = PR_DEV * my_facet + (table_lane >= SUBG).astype(jnp.int32)
    row_tone = table_block * (N_IMG // row_blocks) + (table_lane & (SUBG - 1))
    row_scale = 0.5 * total_rows ** (-0.5)
    for f in range(facet_count):
        start = vis_recv[f * sub_count][5:6, :].astype(jnp.int32)
        rc, rs = table((start + iota((total_rows, LANES), 0)) * row_tone)
        rc = rc * row_scale
        rs = rs * row_scale
        at = slice(f * total_rows, (f + 1) * total_rows)
        row_wide[at, :LANES] = rc.astype(BF16)
        row_wide[at, LANES:] = rs.astype(BF16)
        row_tall[:LANES, at] = rc.T.astype(BF16)
        row_tall[LANES:, at] = rs.T.astype(BF16)
    for j in range(slots // LANES):
        merged = vis_recv[j * group]
        for i in range(1, group):
            merged = merged + vis_recv[j * group + i]
        known[:, j * LANES : (j + 1) * LANES] = merged

    factor = SUBG ** (-0.5)

    @pl.loop(0, slots // CHUNK)
    def bases(c):
        at = pl.ds(pl.multiple_of(c * CHUNK, CHUNK), CHUNK)
        grid = iota((SUBG, CHUNK), 0).astype(F32) * (1.0 / SUBG)
        lr, li = cos_sin(known[0:1, at] * grid)
        left_real[:, at] = lr * factor
        left_imag[:, at] = li * factor
        rr, ri = cos_sin(known[1:2, at] * grid)
        rr = rr * factor
        ri = ri * factor
        basis_one[:, at] = jnp.concatenate([rr, -ri], 0).astype(BF16)
        basis_two[:, at] = jnp.concatenate([ri, rr], 0).astype(BF16)

    wait_all(recv_sems, 1, spec_recv)
    spectra = spec_recv[...].reshape(facet_count * total_rows, LANES)
    both = dot(row_tall[...], spectra)
    half = iota((1, LANES), 1) < SUBG
    turned = pltpu.roll(both[LANES:], SUBG, 1)
    subgrids = both[:LANES] + jnp.where(half, -turned, turned)
    subgrids = subgrids.astype(BF16)
    acc_out = jnp.zeros((LANES, LANES), F32)
    copies = CHUNK // LANES
    for c in range(slots // CHUNK):
        at = slice(c * CHUNK, (c + 1) * CHUNK)
        lr = left_real[:, at]
        li = left_imag[:, at]
        one = basis_one[:, at]
        two = basis_two[:, at]
        slot_lane = iota((1, CHUNK), 1) & (span - 1)
        second = slot_lane >= most
        inner_real = dot(subgrids, one)
        inner_imag = dot(subgrids, two)
        inner_real = jnp.where(second, inner_real[SUBG:], inner_real[:SUBG])
        inner_imag = jnp.where(second, inner_imag[SUBG:], inner_imag[:SUBG])
        level = known[4:5, at]
        live = jnp.where(level > 0.0, 1.0, 0.0)
        misfit_real = known[2:3, at] - jnp.sum(lr * inner_real - li * inner_imag, 0, keepdims=True)
        misfit_imag = known[3:4, at] - jnp.sum(lr * inner_imag + li * inner_real, 0, keepdims=True)
        threshold = level + (1.0 - live)
        magnitude = jnp.sqrt(misfit_real * misfit_real + misfit_imag * misfit_imag)
        weight = live * threshold / jnp.maximum(magnitude, threshold)
        wr = weight * misfit_real
        wi = weight * misfit_imag
        blank = jnp.zeros((6, LANES), F32)
        for k in range(copies):
            part = slice(k * LANES, (k + 1) * LANES)
            back_send[c * copies + k] = jnp.concatenate([wr[:, part], wi[:, part], blank], 0)
        pr = lr * wr + li * wi
        pi = lr * wi - li * wr
        pr = jnp.concatenate([jnp.where(second, 0.0, pr), jnp.where(second, pr, 0.0)], 0)
        pi = jnp.concatenate([jnp.where(second, 0.0, pi), jnp.where(second, pi, 0.0)], 0)
        acc_out = acc_out + dot_nt(pr.astype(BF16), one) + dot_nt(pi.astype(BF16), two)

    gridded = acc_out.astype(BF16).astype(F32)
    turned = pltpu.roll(gridded, SUBG, 1)
    turned = jnp.where(half, turned, -turned)
    gridded = jnp.concatenate([gridded, turned], 0).astype(BF16)
    parts = dot(row_wide[...], gridded)
    image_send[...] = parts.astype(BF16).reshape(devices, rows, LANES)
    send_all(3, lambda f, s: image_send.at[f * sub_count + s], image_recv)
    send_all(2, lambda f, s: back_send.at[lax.div(f * sub_count + s, group)], back_recv)
    image_recv[me] = image_send[me]
    back_recv[me] = back_send[lax.div(me, group)]

    wait_all(recv_sems, 2, back_recv)
    returned = back_recv[...].reshape(devices * 8, LANES)
    found = jnp.zeros((devices * 8, vis), F32)
    for part in three_parts(returned):
        found = found + dot(part, place_ref[...])
    chosen = iota((devices, 8, vis), 0).astype(F32) == owner_ref[...][None]
    found = jnp.sum(jnp.where(chosen, found.reshape(devices, 8, vis), 0.0), 0)
    residual_ref[...] = found[0:2]

    wait_all(recv_sems, 3, image_recv)
    held = image_recv[...].astype(F32).reshape(facet_count, columns * rows, LANES)
    images = held[0]
    for f in range(1, facet_count):
        images = images + held[f]
    image_ref[...] = images

    wait_all(send_sems, 0, vis_recv)
    wait_all(send_sems, 1, spec_recv)
    wait_all(send_sems, 2, back_recv)
    wait_all(send_sems, 3, image_recv)


def adjoint_kernel(
    columns,
    width,
    offsets_ref,
    image_ref,
    found_ref,
    adjoint_ref,
    residual_ref,
    matrix,
    step_cos,
    step_sin,
    straight,
    crossed,
):
    rows = adjoint_ref.shape[2]
    block_steps = adjoint_ref.shape[3] // LANES

    @pl.when(pl.program_id(0) == 0)
    def first():
        residual_ref[...] = found_ref[...]
        column_tables(offsets_ref[0, 1], columns, width, matrix, step_cos, step_sin)
        for q in range(columns):
            image = image_ref[q * rows : (q + 1) * rows, :]
            at = slice(q * LANES, (q + 1) * LANES)
            straight[:, at] = image
            crossed[:, at] = pltpu.roll(image, SUBG, 1)

    start = pl.program_id(0) * block_steps
    pieces = []
    for h in range(block_steps):
        sc = step_cos[pl.ds(start + h, 1), :]
        ss = step_sin[pl.ds(start + h, 1), :]
        piece = []
        for q in range(columns):
            at = slice(q * LANES, (q + 1) * LANES)
            piece.append((straight[:, at] * sc + crossed[:, at] * ss).astype(BF16))
        pieces.append(jnp.concatenate(piece, 1))
    out = dot_nt(jnp.concatenate(pieces, 0), matrix[...])
    for h in range(block_steps):
        at = slice(h * LANES, (h + 1) * LANES)
        adjoint_ref[0, 0, :, at] = out[h * rows : (h + 1) * rows, :LANES]
        adjoint_ref[0, 1, :, at] = out[h * rows : (h + 1) * rows, LANES:]


def on_device(
    facet_slab, facet_offsets, visibility_position, observed, visibility_subgrid, clip_levels
):
    sub_count = lax.axis_size("sub")
    facet_count = lax.axis_size("facet")
    devices = sub_count * facet_count
    rows = facet_slab.shape[2]
    width = facet_slab.shape[3]
    vis = visibility_position.shape[1]
    most = max(2, 2 * vis // (PR_DEV * facet_count * sub_count))
    slots = devices * PR_DEV * most
    all_rows = devices * rows
    vmem = pl.BlockSpec(memory_space=pltpu.VMEM)
    smem = pl.BlockSpec(memory_space=pltpu.SMEM)
    images, found = pl.pallas_call(
        functools.partial(kernel, facet_count, sub_count),
        out_shape=(
            jax.ShapeDtypeStruct((sub_count * rows, LANES), F32),
            jax.ShapeDtypeStruct((2, vis), F32),
        ),
        in_specs=[smem] + [vmem] * 5,
        out_specs=(vmem, vmem),
        scratch_shapes=[
            pltpu.VMEM((devices, 8, LANES), F32),
            pltpu.VMEM((devices, 8, LANES), F32),
            pltpu.VMEM((sub_count, rows, LANES), BF16),
            pltpu.VMEM((devices, rows, LANES), BF16),
            pltpu.VMEM((slots // LANES, 8, LANES), F32),
            pltpu.VMEM((devices, 8, LANES), F32),
            pltpu.VMEM((devices, rows, LANES), BF16),
            pltpu.VMEM((devices, rows, LANES), BF16),
            pltpu.VMEM((LANES, vis), BF16),
            pltpu.VMEM((1, vis), F32),
            pltpu.VMEM((width // LANES * rows, 2 * LANES), BF16),
            pltpu.VMEM((2 * LANES, sub_count * LANES), BF16),
            pltpu.VMEM((width // LANES, LANES), F32),
            pltpu.VMEM((width // LANES, LANES), F32),
            pltpu.VMEM((all_rows, 2 * LANES), BF16),
            pltpu.VMEM((2 * LANES, all_rows), BF16),
            pltpu.VMEM((SUBG, slots), F32),
            pltpu.VMEM((SUBG, slots), F32),
            pltpu.VMEM((2 * SUBG, slots), BF16),
            pltpu.VMEM((2 * SUBG, slots), BF16),
            pltpu.VMEM((8, slots), F32),
            pltpu.SemaphoreType.DMA((4,)),
            pltpu.SemaphoreType.DMA((4,)),
        ],
        compiler_params=pltpu.CompilerParams(
            collective_id=0, has_side_effects=True, vmem_limit_bytes=56 * 1024 * 1024
        ),
    )(
        facet_offsets,
        facet_slab,
        visibility_position,
        observed,
        visibility_subgrid.reshape(1, vis),
        clip_levels.reshape(1, -1),
    )
    blocks = 4
    whole = lambda *shape: pl.BlockSpec(shape, lambda i: (0,) * len(shape))
    return pl.pallas_call(
        functools.partial(adjoint_kernel, sub_count, width),
        grid=(blocks,),
        out_shape=(
            jax.ShapeDtypeStruct(facet_slab.shape, F32),
            jax.ShapeDtypeStruct((2, vis), F32),
        ),
        in_specs=[smem, whole(sub_count * rows, LANES), whole(2, vis)],
        out_specs=(
            pl.BlockSpec((1, 2, rows, width // blocks), lambda i: (0, 0, 0, i)),
            whole(2, vis),
        ),
        scratch_shapes=[
            pltpu.VMEM((2 * LANES, sub_count * LANES), BF16),
            pltpu.VMEM((width // LANES, LANES), F32),
            pltpu.VMEM((width // LANES, LANES), F32),
            pltpu.VMEM((rows, sub_count * LANES), F32),
            pltpu.VMEM((rows, sub_count * LANES), F32),
        ],
        compiler_params=pltpu.CompilerParams(vmem_limit_bytes=32 * 1024 * 1024),
    )(facet_offsets, images, found)


def solution(mesh):
    placed = (
        P("facet", None, "sub", None),
        P("facet", None),
        P(None, ("facet", "sub")),
        P(None, ("facet", "sub")),
        P(("facet", "sub"), None),
        P(("facet", "sub")),
    )
    return jax.shard_map(
        on_device,
        mesh=mesh,
        in_specs=placed,
        out_specs=(P("facet", None, "sub", None), P(None, ("facet", "sub"))),
        check_vma=False,
    )
```

```python
import functools
import math

import jax
import jax.numpy as jnp
from jax import lax
from jax.experimental import pallas as pl
from jax.experimental.pallas import tpu as pltpu
from jax.sharding import PartitionSpec as P

N_IMG = 32768
SUBG = 64
PR_DEV = 2
VIS_BLOCK = 32
LANES = 128
CHUNK = 512

TWO_PI = 2.0 * math.pi
MESH = pl.DeviceIdType.MESH
F32 = jnp.float32
BF16 = jnp.bfloat16


def cos_sin(turns):
    quarter = jnp.floor(turns * 4.0 + 0.5)
    y = (turns - quarter * 0.25) * TWO_PI
    y2 = y * y
    s = y * (1.0 + y2 * (-1 / 6 + y2 * (1 / 120 + y2 * (-1 / 5040 + y2 * (1 / 362880)))))
    c = 1.0 + y2 * (-0.5 + y2 * (1 / 24 + y2 * (-1 / 720 + y2 * (1 / 40320))))
    k = quarter.astype(jnp.int32)
    odd = (k & 1) == 1
    cos = jnp.where(odd, s, c)
    sin = jnp.where(odd, c, s)
    cos = jnp.where(((k + 1) & 2) == 2, -cos, cos)
    sin = jnp.where((k & 2) == 2, -sin, sin)
    return cos, sin


def table(index):
    return cos_sin((index & (N_IMG - 1)).astype(F32) * (-1.0 / N_IMG))


def iota(shape, dim):
    return lax.broadcasted_iota(jnp.int32, shape, dim)


def dot(a, b):
    return jnp.dot(a, b, preferred_element_type=F32)


def dot_nt(a, b):
    return lax.dot_general(a, b, (((1,), (1,)), ((), ())), preferred_element_type=F32)


def dot_tn(a, b):
    return lax.dot_general(a, b, (((0,), (0,)), ((), ())), preferred_element_type=F32)


def three_parts(x):
    high = x.astype(BF16)
    rest = x - high.astype(F32)
    middle = rest.astype(BF16)
    low = (rest - middle.astype(F32)).astype(BF16)
    return high, middle, low


def column_tables(col_offset, columns, width, matrix_ref, step_cos, step_sin):
    lane = iota((LANES, LANES), 1)
    first_half = lane < SUBG
    base_cos, base_sin = table((col_offset + iota((LANES, LANES), 0)) * (lane & (SUBG - 1)))
    scale = width ** (-0.5)
    base_one = jnp.where(first_half, base_cos, base_sin) * scale
    base_two = jnp.where(first_half, -base_sin, base_cos) * scale
    coarse_step = N_IMG // columns
    residue = (col_offset + iota((columns, LANES), 0)) & (columns - 1)
    for q in range(columns):
        cc, cs = table(residue * (q * coarse_step))
        cc = jnp.concatenate([cc] * (LANES // columns), 0)
        cs = jnp.concatenate([cs] * (LANES // columns), 0)
        at = slice(q * LANES, (q + 1) * LANES)
        matrix_ref[:LANES, at] = (cc * base_one + cs * base_two).astype(BF16)
        matrix_ref[LANES:, at] = (cc * base_two - cs * base_one).astype(BF16)
    steps = width // LANES
    step_lane = iota((steps, LANES), 1)
    sc, ss = table(iota((steps, LANES), 0) * LANES * (step_lane & (SUBG - 1)))
    step_cos[...] = sc
    step_sin[...] = jnp.where(step_lane < SUBG, ss, -ss)


def kernel(
    facet_count,
    sub_count,
    offsets_ref,
    slab_ref,
    position_ref,
    observed_ref,
    subgrid_ref,
    clip_ref,
    image_ref,
    residual_ref,
    vis_send,
    vis_recv,
    spec_send,
    spec_stage,
    spec_recv,
    back_send,
    back_recv,
    image_send,
    image_stage,
    image_sum,
    image_recv,
    place_ref,
    owner_ref,
    slab_rows,
    matrix,
    step_cos,
    step_sin,
    row_wide,
    row_tall,
    left_real,
    left_imag,
    basis_one,
    basis_two,
    known,
    send_sems,
    recv_sems,
):
    devices = facet_count * sub_count
    my_facet = lax.axis_index("facet")
    my_sub = lax.axis_index("sub")
    me = my_facet * sub_count + my_sub
    columns = sub_count
    rows = slab_ref.shape[2]
    width = slab_ref.shape[3]
    vis = position_ref.shape[1]
    row_blocks = PR_DEV * facet_count
    most = max(2, 2 * vis // (row_blocks * columns))
    span = PR_DEV * most
    group = LANES // span
    slots = devices * span
    total_rows = rows * sub_count

    partners = []
    for df in range(facet_count):
        facet = my_facet + df
        facet = jnp.where(facet >= facet_count, facet - facet_count, facet)
        for ds in range(sub_count):
            sub = my_sub + ds
            sub = jnp.where(sub >= sub_count, sub - sub_count, sub)
            if df or ds:
                partners.append((facet, sub))
    beside = partners[: sub_count - 1]
    across = partners[sub_count - 1 :: sub_count]

    barrier = pltpu.get_barrier_semaphore()
    for where in partners:
        pl.semaphore_signal(barrier, inc=1, device_id=where, device_id_type=MESH)

    def send_all(kind, peers, source_of, target):
        for facet, sub in peers:
            pltpu.make_async_remote_copy(
                src_ref=source_of(facet, sub),
                dst_ref=target,
                send_sem=send_sems.at[kind],
                recv_sem=recv_sems.at[kind],
                device_id=(facet, sub),
                device_id_type=MESH,
            ).start()

    def wait_all(sems, kind, target):
        whole = target.at[pl.ds(0, target.shape[0] - 1)]
        pltpu.make_async_copy(whole, whole, sems.at[kind]).wait()

    ids = subgrid_ref[...].astype(F32)
    block_row = jnp.floor((ids + 0.5) * (1.0 / columns))
    block_col = ids - block_row * columns
    pair = jnp.floor((block_row + 0.5) * (1.0 / PR_DEV))
    local = block_row - pair * PR_DEV
    owner = pair * sub_count + block_col
    key = owner * PR_DEV + local
    key_rows = iota((devices * PR_DEV, vis), 0).astype(F32)
    same = jnp.where(key_rows == key, 1.0, 0.0)
    earlier = jnp.where(iota((LANES, LANES), 0) < iota((LANES, LANES), 1), 1.0, 0.0).astype(BF16)
    before = jnp.zeros((devices * PR_DEV, 1), F32)
    ranks = []
    for k in range(vis // LANES):
        block = same[:, k * LANES : (k + 1) * LANES]
        counts = dot(block.astype(BF16), earlier) + before
        ranks.append(jnp.sum(block * counts, 0, keepdims=True))
        before = before + jnp.sum(block, 1, keepdims=True)
    rank = jnp.concatenate(ranks, 1)
    my_place = lax.rem(me, group) * span
    slot = my_place.astype(F32) + local * most + rank
    place = jnp.where(iota((LANES, vis), 0).astype(F32) == slot, 1.0, 0.0).astype(BF16)
    place_ref[...] = place
    owner_ref[...] = owner
    clip = jnp.broadcast_to(clip_ref[...].astype(F32), (8, clip_ref.shape[1]))
    block_start = iota((clip_ref.shape[1], vis), 0) * VIS_BLOCK
    block_at = iota((clip_ref.shape[1], vis), 1)
    in_block = (block_at >= block_start) & (block_at < block_start + VIS_BLOCK)
    spread_out = jnp.where(in_block, 1.0, 0.0).astype(BF16)
    levels = dot(clip.astype(BF16), spread_out)[0:1] * 0.25
    values = jnp.concatenate(
        [position_ref[...], observed_ref[...], levels, jnp.zeros((3, vis), F32)], 0
    )
    chosen = iota((devices, 8, vis), 0).astype(F32) == owner[None]
    packed = jnp.zeros((devices * 8, LANES), F32)
    for part in three_parts(values):
        masked = jnp.where(chosen, part.astype(F32)[None], 0.0)
        masked = masked.reshape(devices * 8, vis).astype(BF16)
        packed = packed + dot_nt(masked, place)
    row_offset = offsets_ref[0, 0].astype(F32)
    packed = packed.reshape(devices, 8, LANES)
    packed = jnp.where(iota((devices, 8, LANES), 1) == 5, row_offset, packed)
    vis_send[...] = packed
    vis_recv[me] = vis_send[me]

    pl.semaphore_wait(barrier, devices - 1)
    send_all(0, partners, lambda f, s: vis_send.at[f * sub_count + s], vis_recv.at[me])

    column_tables(offsets_ref[0, 1], columns, width, matrix, step_cos, step_sin)
    steps = width // LANES
    for h in range(steps):
        part = slice(h * LANES, (h + 1) * LANES)
        for c in range(2):
            slab_rows[h * rows : (h + 1) * rows, c * LANES : (c + 1) * LANES] = slab_ref[
                0, c, :, part
            ]
    taken = 16
    for q in range(0, columns, 2):
        both = matrix[:, q * LANES : (q + 2) * LANES]
        straight = jnp.zeros((rows, 2 * LANES), F32)
        crossed = jnp.zeros((rows, 2 * LANES), F32)
        for h in range(0, steps, taken):
            spread = dot(slab_rows[h * rows : (h + taken) * rows, :], both)
            for k in range(taken):
                piece = spread[k * rows : (k + 1) * rows]
                sc = step_cos[h + k : h + k + 1, :]
                ss = step_sin[h + k : h + k + 1, :]
                straight = straight + piece * jnp.concatenate([sc, sc], 1)
                crossed = crossed + piece * jnp.concatenate([ss, ss], 1)
        for k in range(2):
            part = slice(k * LANES, (k + 1) * LANES)
            spectrum = straight[:, part] + pltpu.roll(crossed[:, part], SUBG, 1)
            spec_send[q + k] = spectrum.astype(BF16)

    send_all(1, beside, lambda f, s: spec_send.at[s], spec_stage.at[my_sub])
    spec_stage[my_sub] = spec_send[my_sub]

    wait_all(recv_sems, 0, vis_recv)
    for j in range(slots // LANES):
        merged = vis_recv[j * group]
        for i in range(1, group):
            merged = merged + vis_recv[j * group + i]
        known[:, j * LANES : (j + 1) * LANES] = merged
    wait_all(recv_sems, 1, spec_stage)
    send_all(4, across, lambda f, s: spec_stage, spec_recv.at[my_facet])
    spec_recv[my_facet] = spec_stage[...]
    table_lane = iota((total_rows, LANES), 1)
    table_block = PR_DEV * my_facet + (table_lane >= SUBG).astype(jnp.int32)
    row_tone = table_block * (N_IMG // row_blocks) + (table_lane & (SUBG - 1))
    row_scale = 0.5 * total_rows ** (-0.5)
    for f in range(facet_count):
        start = vis_recv[f * sub_count][5:6, :].astype(jnp.int32)
        rc, rs = table((start + iota((total_rows, LANES), 0)) * row_tone)
        rc = rc * row_scale
        rs = rs * row_scale
        at = slice(f * total_rows, (f + 1) * total_rows)
        row_wide[at, :LANES] = rc.astype(BF16)
        row_wide[at, LANES:] = rs.astype(BF16)
        row_tall[:LANES, at] = rc.T.astype(BF16)
        row_tall[LANES:, at] = rs.T.astype(BF16)
    factor = SUBG ** (-0.5)

    @pl.loop(0, slots // CHUNK)
    def bases(c):
        at = pl.ds(pl.multiple_of(c * CHUNK, CHUNK), CHUNK)
        grid = iota((SUBG, CHUNK), 0).astype(F32) * (1.0 / SUBG)
        lr, li = cos_sin(known[0:1, at] * grid)
        left_real[:, at] = lr * factor
        left_imag[:, at] = li * factor
        rr, ri = cos_sin(known[1:2, at] * grid)
        rr = rr * factor
        ri = ri * factor
        basis_one[:, at] = jnp.concatenate([rr, -ri], 0).astype(BF16)
        basis_two[:, at] = jnp.concatenate([ri, rr], 0).astype(BF16)

    wait_all(recv_sems, 4, spec_recv)
    spectra = spec_recv[...].reshape(facet_count * total_rows, LANES)
    both = dot(row_tall[...], spectra)
    half = iota((1, LANES), 1) < SUBG
    turned = pltpu.roll(both[LANES:], SUBG, 1)
    subgrids = both[:LANES] + jnp.where(half, -turned, turned)
    subgrids = subgrids.astype(BF16)
    acc_out = jnp.zeros((LANES, LANES), F32)
    copies = CHUNK // LANES
    for c in range(slots // CHUNK):
        at = slice(c * CHUNK, (c + 1) * CHUNK)
        lr = left_real[:, at]
        li = left_imag[:, at]
        one = basis_one[:, at]
        two = basis_two[:, at]
        slot_lane = iota((1, CHUNK), 1) & (span - 1)
        second = slot_lane >= most
        inner_real = dot(subgrids, one)
        inner_imag = dot(subgrids, two)
        inner_real = jnp.where(second, inner_real[SUBG:], inner_real[:SUBG])
        inner_imag = jnp.where(second, inner_imag[SUBG:], inner_imag[:SUBG])
        level = known[4:5, at]
        live = jnp.where(level > 0.0, 1.0, 0.0)
        misfit_real = known[2:3, at] - jnp.sum(lr * inner_real - li * inner_imag, 0, keepdims=True)
        misfit_imag = known[3:4, at] - jnp.sum(lr * inner_imag + li * inner_real, 0, keepdims=True)
        threshold = level + (1.0 - live)
        magnitude = jnp.sqrt(misfit_real * misfit_real + misfit_imag * misfit_imag)
        weight = live * threshold / jnp.maximum(magnitude, threshold)
        wr = weight * misfit_real
        wi = weight * misfit_imag
        for k in range(copies):
            part = slice(k * LANES, (k + 1) * LANES)
            back_send[c * copies + k] = jnp.concatenate([wr[:, part], wi[:, part]], 0)
        pr = lr * wr + li * wi
        pi = lr * wi - li * wr
        pr = jnp.concatenate([jnp.where(second, 0.0, pr), jnp.where(second, pr, 0.0)], 0)
        pi = jnp.concatenate([jnp.where(second, 0.0, pi), jnp.where(second, pi, 0.0)], 0)
        acc_out = acc_out + dot_nt(pr.astype(BF16), one) + dot_nt(pi.astype(BF16), two)

    gridded = acc_out.astype(BF16).astype(F32)
    turned = pltpu.roll(gridded, SUBG, 1)
    turned = jnp.where(half, turned, -turned)
    gridded = jnp.concatenate([gridded, turned], 0).astype(BF16)
    parts = dot(row_wide[...], gridded)
    image_send[...] = parts.astype(BF16).reshape(facet_count, sub_count, rows, LANES)
    send_all(3, across, lambda f, s: image_send.at[f], image_stage.at[my_facet])
    send_all(
        2, partners, lambda f, s: back_send.at[lax.div(f * sub_count + s, group)], back_recv.at[me]
    )
    image_stage[my_facet] = image_send[my_facet]
    back_recv[me] = back_send[lax.div(me, group)]

    wait_all(recv_sems, 3, image_stage)
    images = image_stage[0].astype(F32)
    for f in range(1, facet_count):
        images = images + image_stage[f].astype(F32)
    image_sum[...] = images.astype(BF16)
    send_all(5, beside, lambda f, s: image_sum.at[s], image_recv.at[my_sub])
    image_recv[my_sub] = image_sum[my_sub]

    wait_all(recv_sems, 2, back_recv)
    returned = back_recv[...].reshape(devices * 2, LANES)
    found = jnp.zeros((devices * 2, vis), F32)
    for part in three_parts(returned):
        found = found + dot(part, place_ref[...])
    row = iota((devices * 2, vis), 0).astype(F32)
    wanted = owner_ref[...] * 2.0
    residual_ref[0:1, :] = jnp.sum(jnp.where(row == wanted, found, 0.0), 0, keepdims=True)
    residual_ref[1:2, :] = jnp.sum(jnp.where(row == wanted + 1.0, found, 0.0), 0, keepdims=True)

    wait_all(recv_sems, 5, image_recv)
    image_ref[...] = image_recv[...].astype(F32).reshape(columns * rows, LANES)

    wait_all(send_sems, 0, vis_recv)
    wait_all(send_sems, 1, spec_stage)
    wait_all(send_sems, 2, back_recv)
    wait_all(send_sems, 3, image_stage)
    wait_all(send_sems, 4, spec_recv)
    wait_all(send_sems, 5, image_recv)


def adjoint_kernel(
    columns,
    width,
    offsets_ref,
    image_ref,
    found_ref,
    adjoint_ref,
    residual_ref,
    matrix,
    step_cos,
    step_sin,
    straight,
    crossed,
):
    rows = adjoint_ref.shape[2]
    block_steps = adjoint_ref.shape[3] // LANES

    @pl.when(pl.program_id(0) == 0)
    def first():
        residual_ref[...] = found_ref[...]
        column_tables(offsets_ref[0, 1], columns, width, matrix, step_cos, step_sin)
        for q in range(columns):
            image = image_ref[q * rows : (q + 1) * rows, :]
            at = slice(q * LANES, (q + 1) * LANES)
            straight[:, at] = image
            crossed[:, at] = pltpu.roll(image, SUBG, 1)

    start = pl.program_id(0) * block_steps
    pieces = []
    for h in range(block_steps):
        sc = step_cos[pl.ds(start + h, 1), :]
        ss = step_sin[pl.ds(start + h, 1), :]
        piece = []
        for q in range(columns):
            at = slice(q * LANES, (q + 1) * LANES)
            piece.append((straight[:, at] * sc + crossed[:, at] * ss).astype(BF16))
        pieces.append(jnp.concatenate(piece, 1))
    out = dot_nt(jnp.concatenate(pieces, 0), matrix[...])
    for h in range(block_steps):
        at = slice(h * LANES, (h + 1) * LANES)
        adjoint_ref[0, 0, :, at] = out[h * rows : (h + 1) * rows, :LANES]
        adjoint_ref[0, 1, :, at] = out[h * rows : (h + 1) * rows, LANES:]


def on_device(
    facet_slab, facet_offsets, visibility_position, observed, visibility_subgrid, clip_levels
):
    sub_count = lax.axis_size("sub")
    facet_count = lax.axis_size("facet")
    devices = sub_count * facet_count
    rows = facet_slab.shape[2]
    width = facet_slab.shape[3]
    vis = visibility_position.shape[1]
    most = max(2, 2 * vis // (PR_DEV * facet_count * sub_count))
    slots = devices * PR_DEV * most
    all_rows = devices * rows
    vmem = pl.BlockSpec(memory_space=pltpu.VMEM)
    smem = pl.BlockSpec(memory_space=pltpu.SMEM)
    images, found = pl.pallas_call(
        functools.partial(kernel, facet_count, sub_count),
        out_shape=(
            jax.ShapeDtypeStruct((sub_count * rows, LANES), F32),
            jax.ShapeDtypeStruct((2, vis), F32),
        ),
        in_specs=[smem] + [vmem] * 5,
        out_specs=(vmem, vmem),
        scratch_shapes=[
            pltpu.VMEM((devices, 8, LANES), F32),
            pltpu.VMEM((devices, 8, LANES), F32),
            pltpu.VMEM((sub_count, rows, LANES), BF16),
            pltpu.VMEM((sub_count, rows, LANES), BF16),
            pltpu.VMEM((facet_count, sub_count, rows, LANES), BF16),
            pltpu.VMEM((slots // LANES, 2, LANES), F32),
            pltpu.VMEM((devices, 2, LANES), F32),
            pltpu.VMEM((facet_count, sub_count, rows, LANES), BF16),
            pltpu.VMEM((facet_count, sub_count, rows, LANES), BF16),
            pltpu.VMEM((sub_count, rows, LANES), BF16),
            pltpu.VMEM((sub_count, rows, LANES), BF16),
            pltpu.VMEM((LANES, vis), BF16),
            pltpu.VMEM((1, vis), F32),
            pltpu.VMEM((width // LANES * rows, 2 * LANES), BF16),
            pltpu.VMEM((2 * LANES, sub_count * LANES), BF16),
            pltpu.VMEM((width // LANES, LANES), F32),
            pltpu.VMEM((width // LANES, LANES), F32),
            pltpu.VMEM((all_rows, 2 * LANES), BF16),
            pltpu.VMEM((2 * LANES, all_rows), BF16),
            pltpu.VMEM((SUBG, slots), F32),
            pltpu.VMEM((SUBG, slots), F32),
            pltpu.VMEM((2 * SUBG, slots), BF16),
            pltpu.VMEM((2 * SUBG, slots), BF16),
            pltpu.VMEM((8, slots), F32),
            pltpu.SemaphoreType.DMA((6,)),
            pltpu.SemaphoreType.DMA((6,)),
        ],
        compiler_params=pltpu.CompilerParams(
            collective_id=0, has_side_effects=True, vmem_limit_bytes=56 * 1024 * 1024
        ),
    )(
        facet_offsets,
        facet_slab,
        visibility_position,
        observed,
        visibility_subgrid.reshape(1, vis),
        clip_levels.reshape(1, -1),
    )
    blocks = 4
    whole = lambda *shape: pl.BlockSpec(shape, lambda i: (0,) * len(shape))
    return pl.pallas_call(
        functools.partial(adjoint_kernel, sub_count, width),
        grid=(blocks,),
        out_shape=(
            jax.ShapeDtypeStruct(facet_slab.shape, F32),
            jax.ShapeDtypeStruct((2, vis), F32),
        ),
        in_specs=[smem, whole(sub_count * rows, LANES), whole(2, vis)],
        out_specs=(
            pl.BlockSpec((1, 2, rows, width // blocks), lambda i: (0, 0, 0, i)),
            whole(2, vis),
        ),
        scratch_shapes=[
            pltpu.VMEM((2 * LANES, sub_count * LANES), BF16),
            pltpu.VMEM((width // LANES, LANES), F32),
            pltpu.VMEM((width // LANES, LANES), F32),
            pltpu.VMEM((rows, sub_count * LANES), F32),
            pltpu.VMEM((rows, sub_count * LANES), F32),
        ],
        compiler_params=pltpu.CompilerParams(vmem_limit_bytes=60 * 1024 * 1024),
    )(facet_offsets, images, found)


def solution(mesh):
    placed = (
        P("facet", None, "sub", None),
        P("facet", None),
        P(None, ("facet", "sub")),
        P(None, ("facet", "sub")),
        P(("facet", "sub"), None),
        P(("facet", "sub")),
    )
    return jax.shard_map(
        on_device,
        mesh=mesh,
        in_specs=placed,
        out_specs=(P("facet", None, "sub", None), P(None, ("facet", "sub"))),
        check_vma=False,
    )
```

```python
import functools
import math

import jax
import jax.numpy as jnp
from jax import lax
from jax.experimental import pallas as pl
from jax.experimental.pallas import tpu as pltpu
from jax.sharding import PartitionSpec as P

N_IMG = 32768
SUBG = 64
PR_DEV = 2
VIS_BLOCK = 32
LANES = 128
CHUNK = 512

TWO_PI = 2.0 * math.pi
MESH = pl.DeviceIdType.MESH
F32 = jnp.float32
BF16 = jnp.bfloat16


def cos_sin(turns):
    quarter = jnp.floor(turns * 4.0 + 0.5)
    y = (turns - quarter * 0.25) * TWO_PI
    y2 = y * y
    s = y * (1.0 + y2 * (-1 / 6 + y2 * (1 / 120 + y2 * (-1 / 5040 + y2 * (1 / 362880)))))
    c = 1.0 + y2 * (-0.5 + y2 * (1 / 24 + y2 * (-1 / 720 + y2 * (1 / 40320))))
    k = quarter.astype(jnp.int32)
    odd = (k & 1) == 1
    cos = jnp.where(odd, s, c)
    sin = jnp.where(odd, c, s)
    cos = jnp.where(((k + 1) & 2) == 2, -cos, cos)
    sin = jnp.where((k & 2) == 2, -sin, sin)
    return cos, sin


def table(index):
    return cos_sin((index & (N_IMG - 1)).astype(F32) * (-1.0 / N_IMG))


def spread_rows(first, second):
    c1, s1 = first
    c2, s2 = second
    cos, sin = [], []
    for k in range(c2.shape[0]):
        ck = c2[k : k + 1]
        sk = s2[k : k + 1]
        cos.append(c1 * ck - s1 * sk)
        sin.append(c1 * sk + s1 * ck)
    return jnp.concatenate(cos, 0), jnp.concatenate(sin, 0)


def iota(shape, dim):
    return lax.broadcasted_iota(jnp.int32, shape, dim)


def dot(a, b):
    return jnp.dot(a, b, preferred_element_type=F32)


def dot_nt(a, b):
    return lax.dot_general(a, b, (((1,), (1,)), ((), ())), preferred_element_type=F32)


def dot_tn(a, b):
    return lax.dot_general(a, b, (((0,), (0,)), ((), ())), preferred_element_type=F32)


def three_parts(x):
    high = x.astype(BF16)
    rest = x - high.astype(F32)
    middle = rest.astype(BF16)
    low = (rest - middle.astype(F32)).astype(BF16)
    return high, middle, low


def column_tables(col_offset, columns, width, matrix_ref, step_cos, step_sin):
    lane = iota((LANES, LANES), 1)
    first_half = lane < SUBG
    near = (col_offset + iota((8, LANES), 0)) * (iota((8, LANES), 1) & (SUBG - 1))
    blocks = (LANES // 8, LANES)
    far = iota(blocks, 0) * 8 * (iota(blocks, 1) & (SUBG - 1))
    base_cos, base_sin = spread_rows(table(near), table(far))
    scale = width ** (-0.5)
    base_one = jnp.where(first_half, base_cos, base_sin) * scale
    base_two = jnp.where(first_half, -base_sin, base_cos) * scale
    coarse_step = N_IMG // columns
    residue = (col_offset + iota((columns, LANES), 0)) & (columns - 1)
    for q in range(columns):
        cc, cs = table(residue * (q * coarse_step))
        cc = jnp.concatenate([cc] * (LANES // columns), 0)
        cs = jnp.concatenate([cs] * (LANES // columns), 0)
        at = slice(q * LANES, (q + 1) * LANES)
        matrix_ref[:LANES, at] = (cc * base_one + cs * base_two).astype(BF16)
        matrix_ref[LANES:, at] = (cc * base_two - cs * base_one).astype(BF16)
    steps = width // LANES
    step_lane = iota((steps, LANES), 1)
    sc, ss = table(iota((steps, LANES), 0) * LANES * (step_lane & (SUBG - 1)))
    step_cos[...] = sc
    step_sin[...] = jnp.where(step_lane < SUBG, ss, -ss)


def kernel(
    facet_count,
    sub_count,
    offsets_ref,
    slab_ref,
    position_ref,
    observed_ref,
    subgrid_ref,
    clip_ref,
    image_ref,
    residual_ref,
    start_send,
    start_recv,
    vis_send,
    vis_recv,
    spec_send,
    spec_stage,
    spec_recv,
    back_send,
    back_recv,
    image_send,
    image_stage,
    image_sum,
    image_recv,
    place_ref,
    owner_ref,
    slab_rows,
    matrix,
    step_cos,
    step_sin,
    row_wide,
    row_tall,
    left_real,
    left_imag,
    basis_one,
    basis_two,
    known,
    send_sems,
    recv_sems,
):
    devices = facet_count * sub_count
    my_facet = lax.axis_index("facet")
    my_sub = lax.axis_index("sub")
    me = my_facet * sub_count + my_sub
    columns = sub_count
    rows = slab_ref.shape[2]
    width = slab_ref.shape[3]
    vis = position_ref.shape[1]
    row_blocks = PR_DEV * facet_count
    most = max(2, 2 * vis // (row_blocks * columns))
    span = PR_DEV * most
    group = LANES // span
    slots = devices * span
    total_rows = rows * sub_count

    partners = []
    for df in range(facet_count):
        facet = my_facet + df
        facet = jnp.where(facet >= facet_count, facet - facet_count, facet)
        for ds in range(sub_count):
            sub = my_sub + ds
            sub = jnp.where(sub >= sub_count, sub - sub_count, sub)
            if df or ds:
                partners.append((facet, sub))
    beside = partners[: sub_count - 1]
    across = partners[sub_count - 1 :: sub_count]

    barrier = pltpu.get_barrier_semaphore()
    for where in partners:
        pl.semaphore_signal(barrier, inc=1, device_id=where, device_id_type=MESH)

    def send_all(kind, peers, source_of, target):
        for facet, sub in peers:
            pltpu.make_async_remote_copy(
                src_ref=source_of(facet, sub),
                dst_ref=target,
                send_sem=send_sems.at[kind],
                recv_sem=recv_sems.at[kind],
                device_id=(facet, sub),
                device_id_type=MESH,
            ).start()

    def wait_all(sems, kind, target):
        whole = target.at[pl.ds(0, target.shape[0] - 1)]
        pltpu.make_async_copy(whole, whole, sems.at[kind]).wait()

    column_tables(offsets_ref[0, 1], columns, width, matrix, step_cos, step_sin)
    steps = width // LANES
    for h in range(steps):
        part = slice(h * LANES, (h + 1) * LANES)
        for c in range(2):
            slab_rows[h * rows : (h + 1) * rows, c * LANES : (c + 1) * LANES] = slab_ref[
                0, c, :, part
            ]
    taken = 16
    for q in range(0, columns, 2):
        both = matrix[:, q * LANES : (q + 2) * LANES]
        straight = jnp.zeros((rows, 2 * LANES), F32)
        crossed = jnp.zeros((rows, 2 * LANES), F32)
        for h in range(0, steps, taken):
            spread = dot(slab_rows[h * rows : (h + taken) * rows, :], both)
            for k in range(taken):
                piece = spread[k * rows : (k + 1) * rows]
                sc = step_cos[h + k : h + k + 1, :]
                ss = step_sin[h + k : h + k + 1, :]
                straight = straight + piece * jnp.concatenate([sc, sc], 1)
                crossed = crossed + piece * jnp.concatenate([ss, ss], 1)
        for k in range(2):
            part = slice(k * LANES, (k + 1) * LANES)
            spectrum = straight[:, part] + pltpu.roll(crossed[:, part], SUBG, 1)
            spec_send[q + k] = spectrum.astype(BF16)

    start_send[...] = jnp.zeros(start_send.shape, F32) + offsets_ref[0, 0].astype(F32)
    pl.semaphore_wait(barrier, devices - 1)
    send_all(1, beside, lambda f, s: spec_send.at[s], spec_stage.at[my_sub])
    spec_stage[my_sub] = spec_send[my_sub]
    send_all(6, across, lambda f, s: start_send, start_recv.at[my_facet])
    start_recv[my_facet] = start_send[...]

    ids = subgrid_ref[...].astype(F32)
    block_row = jnp.floor((ids + 0.5) * (1.0 / columns))
    block_col = ids - block_row * columns
    pair = jnp.floor((block_row + 0.5) * (1.0 / PR_DEV))
    local = block_row - pair * PR_DEV
    owner = pair * sub_count + block_col
    key = owner * PR_DEV + local
    key_rows = iota((devices * PR_DEV, vis), 0).astype(F32)
    same = jnp.where(key_rows == key, 1.0, 0.0)
    earlier = jnp.where(iota((LANES, LANES), 0) < iota((LANES, LANES), 1), 1.0, 0.0).astype(BF16)
    before = jnp.zeros((devices * PR_DEV, 1), F32)
    ranks = []
    for k in range(vis // LANES):
        block = same[:, k * LANES : (k + 1) * LANES]
        counts = dot(block.astype(BF16), earlier) + before
        ranks.append(jnp.sum(block * counts, 0, keepdims=True))
        before = before + jnp.sum(block, 1, keepdims=True)
    rank = jnp.concatenate(ranks, 1)
    my_place = lax.rem(me, group) * span
    slot = my_place.astype(F32) + local * most + rank
    place = jnp.where(iota((LANES, vis), 0).astype(F32) == slot, 1.0, 0.0).astype(BF16)
    place_ref[...] = place
    owner_ref[...] = owner
    clip = jnp.broadcast_to(clip_ref[...].astype(F32), (8, clip_ref.shape[1]))
    block_start = iota((clip_ref.shape[1], vis), 0) * VIS_BLOCK
    block_at = iota((clip_ref.shape[1], vis), 1)
    in_block = (block_at >= block_start) & (block_at < block_start + VIS_BLOCK)
    spread_out = jnp.where(in_block, 1.0, 0.0).astype(BF16)
    levels = dot(clip.astype(BF16), spread_out)[0:1] * 0.25
    values = jnp.concatenate(
        [position_ref[...], observed_ref[...], levels, jnp.zeros((3, vis), F32)], 0
    )
    chosen = iota((devices, 8, vis), 0).astype(F32) == owner[None]
    packed = jnp.zeros((devices * 8, LANES), F32)
    for part in three_parts(values):
        masked = jnp.where(chosen, part.astype(F32)[None], 0.0)
        masked = masked.reshape(devices * 8, vis).astype(BF16)
        packed = packed + dot_nt(masked, place)
    vis_send[...] = packed.reshape(devices, 8, LANES)
    send_all(0, partners, lambda f, s: vis_send.at[f * sub_count + s], vis_recv.at[me])
    vis_recv[me] = vis_send[me]

    wait_all(recv_sems, 1, spec_stage)
    send_all(4, across, lambda f, s: spec_stage, spec_recv.at[my_facet])
    spec_recv[my_facet] = spec_stage[...]

    def row_tone(shape):
        at = iota(shape, 1)
        block = PR_DEV * my_facet + (at >= SUBG).astype(jnp.int32)
        return block * (N_IMG // row_blocks) + (at & (SUBG - 1))

    row_scale = 0.5 * total_rows ** (-0.5)
    blocks = (total_rows // 8, LANES)
    far = table(iota(blocks, 0) * 8 * row_tone(blocks))
    wait_all(recv_sems, 6, start_recv)
    for f in range(facet_count):
        start = start_recv[f].astype(jnp.int32)
        rc, rs = table((start + iota((8, LANES), 0)) * row_tone((8, LANES)))
        rc, rs = spread_rows((rc * row_scale, rs * row_scale), far)
        at = slice(f * total_rows, (f + 1) * total_rows)
        row_wide[at, :LANES] = rc.astype(BF16)
        row_wide[at, LANES:] = rs.astype(BF16)
        row_tall[:LANES, at] = rc.T.astype(BF16)
        row_tall[LANES:, at] = rs.T.astype(BF16)

    wait_all(recv_sems, 0, vis_recv)
    for j in range(slots // LANES):
        merged = vis_recv[j * group]
        for i in range(1, group):
            merged = merged + vis_recv[j * group + i]
        known[:, j * LANES : (j + 1) * LANES] = merged

    factor = SUBG ** (-0.5)

    for c in range(slots // CHUNK):
        at = slice(c * CHUNK, (c + 1) * CHUNK)
        near = iota((8, CHUNK), 0).astype(F32) * (1.0 / SUBG)
        far = iota((SUBG // 8, CHUNK), 0).astype(F32) * (8.0 / SUBG)
        u = known[0:1, at]
        w = known[1:2, at]
        lr, li = spread_rows(cos_sin(u * near), cos_sin(u * far))
        left_real[:, at] = lr * factor
        left_imag[:, at] = li * factor
        rr, ri = spread_rows(cos_sin(w * near), cos_sin(w * far))
        rr = rr * factor
        ri = ri * factor
        basis_one[:, at] = jnp.concatenate([rr, -ri], 0).astype(BF16)
        basis_two[:, at] = jnp.concatenate([ri, rr], 0).astype(BF16)

    wait_all(recv_sems, 4, spec_recv)
    spectra = spec_recv[...].reshape(facet_count * total_rows, LANES)
    both = dot(row_tall[...], spectra)
    half = iota((1, LANES), 1) < SUBG
    turned = pltpu.roll(both[LANES:], SUBG, 1)
    subgrids = both[:LANES] + jnp.where(half, -turned, turned)
    subgrids = subgrids.astype(BF16)
    acc_out = jnp.zeros((LANES, LANES), F32)
    copies = CHUNK // LANES
    for c in range(slots // CHUNK):
        at = slice(c * CHUNK, (c + 1) * CHUNK)
        lr = left_real[:, at]
        li = left_imag[:, at]
        one = basis_one[:, at]
        two = basis_two[:, at]
        slot_lane = iota((1, CHUNK), 1) & (span - 1)
        second = slot_lane >= most
        inner_real = dot(subgrids, one)
        inner_imag = dot(subgrids, two)
        inner_real = jnp.where(second, inner_real[SUBG:], inner_real[:SUBG])
        inner_imag = jnp.where(second, inner_imag[SUBG:], inner_imag[:SUBG])
        level = known[4:5, at]
        live = jnp.where(level > 0.0, 1.0, 0.0)
        misfit_real = known[2:3, at] - jnp.sum(lr * inner_real - li * inner_imag, 0, keepdims=True)
        misfit_imag = known[3:4, at] - jnp.sum(lr * inner_imag + li * inner_real, 0, keepdims=True)
        threshold = level + (1.0 - live)
        magnitude = jnp.sqrt(misfit_real * misfit_real + misfit_imag * misfit_imag)
        weight = live * threshold / jnp.maximum(magnitude, threshold)
        wr = weight * misfit_real
        wi = weight * misfit_imag
        for k in range(copies):
            part = slice(k * LANES, (k + 1) * LANES)
            back_send[c * copies + k] = jnp.concatenate([wr[:, part], wi[:, part]], 0)
        pr = lr * wr + li * wi
        pi = lr * wi - li * wr
        pr = jnp.concatenate([jnp.where(second, 0.0, pr), jnp.where(second, pr, 0.0)], 0)
        pi = jnp.concatenate([jnp.where(second, 0.0, pi), jnp.where(second, pi, 0.0)], 0)
        acc_out = acc_out + dot_nt(pr.astype(BF16), one) + dot_nt(pi.astype(BF16), two)

    gridded = acc_out.astype(BF16).astype(F32)
    turned = pltpu.roll(gridded, SUBG, 1)
    turned = jnp.where(half, turned, -turned)
    gridded = jnp.concatenate([gridded, turned], 0).astype(BF16)
    parts = dot(row_wide[...], gridded)
    image_send[...] = parts.astype(BF16).reshape(facet_count, sub_count, rows, LANES)
    send_all(3, across, lambda f, s: image_send.at[f], image_stage.at[my_facet])
    send_all(
        2, partners, lambda f, s: back_send.at[lax.div(f * sub_count + s, group)], back_recv.at[me]
    )
    image_stage[my_facet] = image_send[my_facet]
    back_recv[me] = back_send[lax.div(me, group)]

    wait_all(recv_sems, 3, image_stage)
    images = image_stage[0].astype(F32)
    for f in range(1, facet_count):
        images = images + image_stage[f].astype(F32)
    image_sum[...] = images.astype(BF16)
    send_all(5, beside, lambda f, s: image_sum.at[s], image_recv.at[my_sub])
    image_recv[my_sub] = image_sum[my_sub]

    wait_all(recv_sems, 2, back_recv)
    returned = back_recv[...].reshape(devices * 2, LANES)
    found = jnp.zeros((devices * 2, vis), F32)
    for part in three_parts(returned):
        found = found + dot(part, place_ref[...])
    row = iota((devices * 2, vis), 0).astype(F32)
    wanted = owner_ref[...] * 2.0
    residual_ref[0:1, :] = jnp.sum(jnp.where(row == wanted, found, 0.0), 0, keepdims=True)
    residual_ref[1:2, :] = jnp.sum(jnp.where(row == wanted + 1.0, found, 0.0), 0, keepdims=True)

    wait_all(recv_sems, 5, image_recv)
    image_ref[...] = image_recv[...].astype(F32).reshape(columns * rows, LANES)

    wait_all(send_sems, 0, vis_recv)
    wait_all(send_sems, 1, spec_stage)
    wait_all(send_sems, 2, back_recv)
    wait_all(send_sems, 3, image_stage)
    wait_all(send_sems, 4, spec_recv)
    wait_all(send_sems, 5, image_recv)
    wait_all(send_sems, 6, start_recv)


def adjoint_kernel(
    columns,
    width,
    offsets_ref,
    image_ref,
    found_ref,
    adjoint_ref,
    residual_ref,
    matrix,
    step_cos,
    step_sin,
    straight,
    crossed,
):
    rows = adjoint_ref.shape[2]
    block_steps = adjoint_ref.shape[3] // LANES

    @pl.when(pl.program_id(0) == 0)
    def first():
        residual_ref[...] = found_ref[...]
        column_tables(offsets_ref[0, 1], columns, width, matrix, step_cos, step_sin)
        for q in range(columns):
            image = image_ref[q * rows : (q + 1) * rows, :]
            at = slice(q * LANES, (q + 1) * LANES)
            straight[:, at] = image
            crossed[:, at] = pltpu.roll(image, SUBG, 1)

    start = pl.program_id(0) * block_steps
    pieces = []
    for h in range(block_steps):
        sc = step_cos[pl.ds(start + h, 1), :]
        ss = step_sin[pl.ds(start + h, 1), :]
        piece = []
        for q in range(columns):
            at = slice(q * LANES, (q + 1) * LANES)
            piece.append((straight[:, at] * sc + crossed[:, at] * ss).astype(BF16))
        pieces.append(jnp.concatenate(piece, 1))
    out = dot_nt(jnp.concatenate(pieces, 0), matrix[...])
    for h in range(block_steps):
        at = slice(h * LANES, (h + 1) * LANES)
        adjoint_ref[0, 0, :, at] = out[h * rows : (h + 1) * rows, :LANES]
        adjoint_ref[0, 1, :, at] = out[h * rows : (h + 1) * rows, LANES:]


def on_device(
    facet_slab, facet_offsets, visibility_position, observed, visibility_subgrid, clip_levels
):
    sub_count = lax.axis_size("sub")
    facet_count = lax.axis_size("facet")
    devices = sub_count * facet_count
    rows = facet_slab.shape[2]
    width = facet_slab.shape[3]
    vis = visibility_position.shape[1]
    most = max(2, 2 * vis // (PR_DEV * facet_count * sub_count))
    slots = devices * PR_DEV * most
    all_rows = devices * rows
    vmem = pl.BlockSpec(memory_space=pltpu.VMEM)
    smem = pl.BlockSpec(memory_space=pltpu.SMEM)
    images, found = pl.pallas_call(
        functools.partial(kernel, facet_count, sub_count),
        out_shape=(
            jax.ShapeDtypeStruct((sub_count * rows, LANES), F32),
            jax.ShapeDtypeStruct((2, vis), F32),
        ),
        in_specs=[smem] + [vmem] * 5,
        out_specs=(vmem, vmem),
        scratch_shapes=[
            pltpu.VMEM((8, LANES), F32),
            pltpu.VMEM((facet_count, 8, LANES), F32),
            pltpu.VMEM((devices, 8, LANES), F32),
            pltpu.VMEM((devices, 8, LANES), F32),
            pltpu.VMEM((sub_count, rows, LANES), BF16),
            pltpu.VMEM((sub_count, rows, LANES), BF16),
            pltpu.VMEM((facet_count, sub_count, rows, LANES), BF16),
            pltpu.VMEM((slots // LANES, 2, LANES), F32),
            pltpu.VMEM((devices, 2, LANES), F32),
            pltpu.VMEM((facet_count, sub_count, rows, LANES), BF16),
            pltpu.VMEM((facet_count, sub_count, rows, LANES), BF16),
            pltpu.VMEM((sub_count, rows, LANES), BF16),
            pltpu.VMEM((sub_count, rows, LANES), BF16),
            pltpu.VMEM((LANES, vis), BF16),
            pltpu.VMEM((1, vis), F32),
            pltpu.VMEM((width // LANES * rows, 2 * LANES), BF16),
            pltpu.VMEM((2 * LANES, sub_count * LANES), BF16),
            pltpu.VMEM((width // LANES, LANES), F32),
            pltpu.VMEM((width // LANES, LANES), F32),
            pltpu.VMEM((all_rows, 2 * LANES), BF16),
            pltpu.VMEM((2 * LANES, all_rows), BF16),
            pltpu.VMEM((SUBG, slots), F32),
            pltpu.VMEM((SUBG, slots), F32),
            pltpu.VMEM((2 * SUBG, slots), BF16),
            pltpu.VMEM((2 * SUBG, slots), BF16),
            pltpu.VMEM((8, slots), F32),
            pltpu.SemaphoreType.DMA((7,)),
            pltpu.SemaphoreType.DMA((7,)),
        ],
        compiler_params=pltpu.CompilerParams(
            collective_id=0, has_side_effects=True, vmem_limit_bytes=56 * 1024 * 1024
        ),
    )(
        facet_offsets,
        facet_slab,
        visibility_position,
        observed,
        visibility_subgrid.reshape(1, vis),
        clip_levels.reshape(1, -1),
    )
    blocks = 4
    whole = lambda *shape: pl.BlockSpec(shape, lambda i: (0,) * len(shape))
    return pl.pallas_call(
        functools.partial(adjoint_kernel, sub_count, width),
        grid=(blocks,),
        out_shape=(
            jax.ShapeDtypeStruct(facet_slab.shape, F32),
            jax.ShapeDtypeStruct((2, vis), F32),
        ),
        in_specs=[smem, whole(sub_count * rows, LANES), whole(2, vis)],
        out_specs=(
            pl.BlockSpec((1, 2, rows, width // blocks), lambda i: (0, 0, 0, i)),
            whole(2, vis),
        ),
        scratch_shapes=[
            pltpu.VMEM((2 * LANES, sub_count * LANES), BF16),
            pltpu.VMEM((width // LANES, LANES), F32),
            pltpu.VMEM((width // LANES, LANES), F32),
            pltpu.VMEM((rows, sub_count * LANES), F32),
            pltpu.VMEM((rows, sub_count * LANES), F32),
        ],
        compiler_params=pltpu.CompilerParams(vmem_limit_bytes=60 * 1024 * 1024),
    )(facet_offsets, images, found)


def solution(mesh):
    placed = (
        P("facet", None, "sub", None),
        P("facet", None),
        P(None, ("facet", "sub")),
        P(None, ("facet", "sub")),
        P(("facet", "sub"), None),
        P(("facet", "sub")),
    )
    return jax.shard_map(
        on_device,
        mesh=mesh,
        in_specs=placed,
        out_specs=(P("facet", None, "sub", None), P(None, ("facet", "sub"))),
        check_vma=False,
    )
```

```python
import functools
import math

import jax
import jax.numpy as jnp
from jax import lax
from jax.experimental import pallas as pl
from jax.experimental.pallas import tpu as pltpu
from jax.sharding import PartitionSpec as P

N_IMG = 32768
SUBG = 64
PR_DEV = 2
VIS_BLOCK = 32
LANES = 128
CHUNK = 512

TWO_PI = 2.0 * math.pi
MESH = pl.DeviceIdType.MESH
F32 = jnp.float32
BF16 = jnp.bfloat16


def cos_sin(turns):
    quarter = jnp.floor(turns * 4.0 + 0.5)
    y = (turns - quarter * 0.25) * TWO_PI
    y2 = y * y
    s = y * (1.0 + y2 * (-1 / 6 + y2 * (1 / 120 + y2 * (-1 / 5040 + y2 * (1 / 362880)))))
    c = 1.0 + y2 * (-0.5 + y2 * (1 / 24 + y2 * (-1 / 720 + y2 * (1 / 40320))))
    k = quarter.astype(jnp.int32)
    odd = (k & 1) == 1
    cos = jnp.where(odd, s, c)
    sin = jnp.where(odd, c, s)
    cos = jnp.where(((k + 1) & 2) == 2, -cos, cos)
    sin = jnp.where((k & 2) == 2, -sin, sin)
    return cos, sin


def table(index):
    return cos_sin((index & (N_IMG - 1)).astype(F32) * (-1.0 / N_IMG))


def spread_rows(first, second):
    c1, s1 = first
    c2, s2 = second
    cos, sin = [], []
    for k in range(c2.shape[0]):
        ck = c2[k : k + 1]
        sk = s2[k : k + 1]
        cos.append(c1 * ck - s1 * sk)
        sin.append(c1 * sk + s1 * ck)
    return jnp.concatenate(cos, 0), jnp.concatenate(sin, 0)


def iota(shape, dim):
    return lax.broadcasted_iota(jnp.int32, shape, dim)


def dot(a, b):
    return jnp.dot(a, b, preferred_element_type=F32)


def dot_nt(a, b):
    return lax.dot_general(a, b, (((1,), (1,)), ((), ())), preferred_element_type=F32)


def dot_tn(a, b):
    return lax.dot_general(a, b, (((0,), (0,)), ((), ())), preferred_element_type=F32)


def three_parts(x):
    high = x.astype(BF16)
    rest = x - high.astype(F32)
    middle = rest.astype(BF16)
    low = (rest - middle.astype(F32)).astype(BF16)
    return high, middle, low


def column_tables(col_offset, columns, width, matrix_ref, step_cos, step_sin):
    lane = iota((LANES, LANES), 1)
    first_half = lane < SUBG
    near = (col_offset + iota((8, LANES), 0)) * (iota((8, LANES), 1) & (SUBG - 1))
    blocks = (LANES // 8, LANES)
    far = iota(blocks, 0) * 8 * (iota(blocks, 1) & (SUBG - 1))
    base_cos, base_sin = spread_rows(table(near), table(far))
    scale = width ** (-0.5)
    base_one = jnp.where(first_half, base_cos, base_sin) * scale
    base_two = jnp.where(first_half, -base_sin, base_cos) * scale
    coarse_step = N_IMG // columns
    residue = (col_offset + iota((columns, LANES), 0)) & (columns - 1)
    for q in range(columns):
        cc, cs = table(residue * (q * coarse_step))
        cc = jnp.concatenate([cc] * (LANES // columns), 0)
        cs = jnp.concatenate([cs] * (LANES // columns), 0)
        at = slice(q * LANES, (q + 1) * LANES)
        matrix_ref[:LANES, at] = (cc * base_one + cs * base_two).astype(BF16)
        matrix_ref[LANES:, at] = (cc * base_two - cs * base_one).astype(BF16)
    steps = width // LANES
    step_lane = iota((steps, LANES), 1)
    sc, ss = table(iota((steps, LANES), 0) * LANES * (step_lane & (SUBG - 1)))
    step_cos[...] = sc
    step_sin[...] = jnp.where(step_lane < SUBG, ss, -ss)


def kernel(
    facet_count,
    sub_count,
    offsets_ref,
    slab_ref,
    position_ref,
    observed_ref,
    subgrid_ref,
    clip_ref,
    image_ref,
    residual_ref,
    start_send,
    start_recv,
    vis_send,
    vis_recv,
    spec_send,
    spec_stage,
    spec_recv,
    back_send,
    back_recv,
    image_send,
    image_stage,
    image_sum,
    image_recv,
    place_ref,
    owner_ref,
    slab_rows,
    matrix,
    step_cos,
    step_sin,
    row_wide,
    row_tall,
    left_real,
    left_imag,
    basis_one,
    basis_two,
    known,
    send_sems,
    recv_sems,
):
    devices = facet_count * sub_count
    my_facet = lax.axis_index("facet")
    my_sub = lax.axis_index("sub")
    me = my_facet * sub_count + my_sub
    columns = sub_count
    rows = slab_ref.shape[2]
    width = slab_ref.shape[3]
    vis = position_ref.shape[1]
    row_blocks = PR_DEV * facet_count
    most = max(2, 2 * vis // (row_blocks * columns))
    span = PR_DEV * most
    group = LANES // span
    slots = devices * span
    total_rows = rows * sub_count

    partners = []
    for df in range(facet_count):
        facet = my_facet + df
        facet = jnp.where(facet >= facet_count, facet - facet_count, facet)
        for ds in range(sub_count):
            sub = my_sub + ds
            sub = jnp.where(sub >= sub_count, sub - sub_count, sub)
            if df or ds:
                partners.append((facet, sub))
    beside = partners[: sub_count - 1]
    across = partners[sub_count - 1 :: sub_count]

    barrier = pltpu.get_barrier_semaphore()
    for where in partners:
        pl.semaphore_signal(barrier, inc=1, device_id=where, device_id_type=MESH)

    def send_all(kind, peers, source_of, target):
        for facet, sub in peers:
            pltpu.make_async_remote_copy(
                src_ref=source_of(facet, sub),
                dst_ref=target,
                send_sem=send_sems.at[kind],
                recv_sem=recv_sems.at[kind],
                device_id=(facet, sub),
                device_id_type=MESH,
            ).start()

    def wait_all(sems, kind, target):
        whole = target.at[pl.ds(0, target.shape[0] - 1)]
        pltpu.make_async_copy(whole, whole, sems.at[kind]).wait()

    column_tables(offsets_ref[0, 1], columns, width, matrix, step_cos, step_sin)
    steps = width // LANES
    for h in range(steps):
        part = slice(h * LANES, (h + 1) * LANES)
        for c in range(2):
            slab_rows[h * rows : (h + 1) * rows, c * LANES : (c + 1) * LANES] = slab_ref[
                0, c, :, part
            ]
    taken = 16
    for q in range(0, columns, 2):
        both = matrix[:, q * LANES : (q + 2) * LANES]
        straight = jnp.zeros((rows, 2 * LANES), F32)
        crossed = jnp.zeros((rows, 2 * LANES), F32)
        for h in range(0, steps, taken):
            spread = dot(slab_rows[h * rows : (h + taken) * rows, :], both)
            for k in range(taken):
                piece = spread[k * rows : (k + 1) * rows]
                sc = step_cos[h + k : h + k + 1, :]
                ss = step_sin[h + k : h + k + 1, :]
                straight = straight + piece * jnp.concatenate([sc, sc], 1)
                crossed = crossed + piece * jnp.concatenate([ss, ss], 1)
        for k in range(2):
            part = slice(k * LANES, (k + 1) * LANES)
            spectrum = straight[:, part] + pltpu.roll(crossed[:, part], SUBG, 1)
            spec_send[q + k] = spectrum.astype(BF16)

    start_send[...] = jnp.zeros(start_send.shape, F32) + offsets_ref[0, 0].astype(F32)
    pl.semaphore_wait(barrier, devices - 1)
    send_all(1, beside, lambda f, s: spec_send.at[s], spec_stage.at[my_sub])
    spec_stage[my_sub] = spec_send[my_sub]
    send_all(6, across, lambda f, s: start_send, start_recv.at[my_facet])
    start_recv[my_facet] = start_send[...]

    ids = subgrid_ref[...].astype(F32)
    block_row = jnp.floor((ids + 0.5) * (1.0 / columns))
    block_col = ids - block_row * columns
    pair = jnp.floor((block_row + 0.5) * (1.0 / PR_DEV))
    local = block_row - pair * PR_DEV
    owner = pair * sub_count + block_col
    key = owner * PR_DEV + local
    key_rows = iota((devices * PR_DEV, vis), 0).astype(F32)
    same = jnp.where(key_rows == key, 1.0, 0.0)
    earlier = jnp.where(iota((LANES, LANES), 0) < iota((LANES, LANES), 1), 1.0, 0.0).astype(BF16)
    before = jnp.zeros((devices * PR_DEV, 1), F32)
    ranks = []
    for k in range(vis // LANES):
        block = same[:, k * LANES : (k + 1) * LANES]
        counts = dot(block.astype(BF16), earlier) + before
        ranks.append(jnp.sum(block * counts, 0, keepdims=True))
        before = before + jnp.sum(block, 1, keepdims=True)
    rank = jnp.concatenate(ranks, 1)
    my_place = lax.rem(me, group) * span
    slot = my_place.astype(F32) + local * most + rank
    place = jnp.where(iota((LANES, vis), 0).astype(F32) == slot, 1.0, 0.0).astype(BF16)
    place_ref[...] = place
    owner_ref[...] = owner
    clip = jnp.broadcast_to(clip_ref[...].astype(F32), (8, clip_ref.shape[1]))
    block_start = iota((clip_ref.shape[1], vis), 0) * VIS_BLOCK
    block_at = iota((clip_ref.shape[1], vis), 1)
    in_block = (block_at >= block_start) & (block_at < block_start + VIS_BLOCK)
    spread_out = jnp.where(in_block, 1.0, 0.0).astype(BF16)
    levels = dot(clip.astype(BF16), spread_out)[0:1] * 0.25
    high, middle, low = three_parts(jnp.concatenate([position_ref[...], observed_ref[...]], 0))
    values = jnp.concatenate(
        [
            high.astype(F32),
            levels,
            jnp.zeros((3, vis), F32),
            middle.astype(F32),
            low.astype(F32),
        ],
        0,
    )
    chosen = iota((devices, 16, vis), 0).astype(F32) == owner[None]
    masked = jnp.where(chosen, values[None], 0.0).reshape(devices * 16, vis).astype(BF16)
    packed = dot_nt(masked, place).reshape(devices, 16, LANES)
    finer = packed[:, 8:12] + packed[:, 12:16]
    finer = jnp.concatenate([finer, jnp.zeros((devices, 4, LANES), F32)], 1)
    vis_send[...] = packed[:, 0:8] + finer
    send_all(0, partners, lambda f, s: vis_send.at[f * sub_count + s], vis_recv.at[me])
    vis_recv[me] = vis_send[me]

    wait_all(recv_sems, 1, spec_stage)
    send_all(4, across, lambda f, s: spec_stage, spec_recv.at[my_facet])
    spec_recv[my_facet] = spec_stage[...]

    def row_tone(shape):
        at = iota(shape, 1)
        block = PR_DEV * my_facet + (at >= SUBG).astype(jnp.int32)
        return block * (N_IMG // row_blocks) + (at & (SUBG - 1))

    row_scale = 0.5 * total_rows ** (-0.5)
    blocks = (total_rows // 8, LANES)
    far = table(iota(blocks, 0) * 8 * row_tone(blocks))
    wait_all(recv_sems, 6, start_recv)
    for f in range(facet_count):
        start = start_recv[f].astype(jnp.int32)
        rc, rs = table((start + iota((8, LANES), 0)) * row_tone((8, LANES)))
        rc, rs = spread_rows((rc * row_scale, rs * row_scale), far)
        at = slice(f * total_rows, (f + 1) * total_rows)
        row_wide[at, :LANES] = rc.astype(BF16)
        row_wide[at, LANES:] = rs.astype(BF16)
        row_tall[:LANES, at] = rc.T.astype(BF16)
        row_tall[LANES:, at] = rs.T.astype(BF16)

    wait_all(recv_sems, 0, vis_recv)
    for j in range(slots // LANES):
        merged = vis_recv[j * group]
        for i in range(1, group):
            merged = merged + vis_recv[j * group + i]
        known[:, j * LANES : (j + 1) * LANES] = merged

    factor = SUBG ** (-0.5)

    for c in range(slots // CHUNK):
        at = slice(c * CHUNK, (c + 1) * CHUNK)
        near = iota((8, CHUNK), 0).astype(F32) * (1.0 / SUBG)
        far = iota((SUBG // 8, CHUNK), 0).astype(F32) * (8.0 / SUBG)
        u = known[0:1, at]
        w = known[1:2, at]
        lr, li = spread_rows(cos_sin(u * near), cos_sin(u * far))
        left_real[:, at] = lr * factor
        left_imag[:, at] = li * factor
        rr, ri = spread_rows(cos_sin(w * near), cos_sin(w * far))
        rr = rr * factor
        ri = ri * factor
        basis_one[:, at] = jnp.concatenate([rr, -ri], 0).astype(BF16)
        basis_two[:, at] = jnp.concatenate([ri, rr], 0).astype(BF16)

    wait_all(recv_sems, 4, spec_recv)
    spectra = spec_recv[...].reshape(facet_count * total_rows, LANES)
    both = dot(row_tall[...], spectra)
    half = iota((1, LANES), 1) < SUBG
    turned = pltpu.roll(both[LANES:], SUBG, 1)
    subgrids = both[:LANES] + jnp.where(half, -turned, turned)
    subgrids = subgrids.astype(BF16)
    acc_out = jnp.zeros((LANES, LANES), F32)
    copies = CHUNK // LANES
    for c in range(slots // CHUNK):
        at = slice(c * CHUNK, (c + 1) * CHUNK)
        lr = left_real[:, at]
        li = left_imag[:, at]
        one = basis_one[:, at]
        two = basis_two[:, at]
        slot_lane = iota((1, CHUNK), 1) & (span - 1)
        second = slot_lane >= most
        inner_real = dot(subgrids, one)
        inner_imag = dot(subgrids, two)
        inner_real = jnp.where(second, inner_real[SUBG:], inner_real[:SUBG])
        inner_imag = jnp.where(second, inner_imag[SUBG:], inner_imag[:SUBG])
        level = known[4:5, at]
        live = jnp.where(level > 0.0, 1.0, 0.0)
        misfit_real = known[2:3, at] - jnp.sum(lr * inner_real - li * inner_imag, 0, keepdims=True)
        misfit_imag = known[3:4, at] - jnp.sum(lr * inner_imag + li * inner_real, 0, keepdims=True)
        threshold = level + (1.0 - live)
        magnitude = jnp.sqrt(misfit_real * misfit_real + misfit_imag * misfit_imag)
        weight = live * threshold / jnp.maximum(magnitude, threshold)
        wr = weight * misfit_real
        wi = weight * misfit_imag
        for k in range(copies):
            part = slice(k * LANES, (k + 1) * LANES)
            back_send[c * copies + k] = jnp.concatenate([wr[:, part], wi[:, part]], 0)
        pr = lr * wr + li * wi
        pi = lr * wi - li * wr
        pr = jnp.concatenate([jnp.where(second, 0.0, pr), jnp.where(second, pr, 0.0)], 0)
        pi = jnp.concatenate([jnp.where(second, 0.0, pi), jnp.where(second, pi, 0.0)], 0)
        acc_out = acc_out + dot_nt(pr.astype(BF16), one) + dot_nt(pi.astype(BF16), two)

    gridded = acc_out.astype(BF16).astype(F32)
    turned = pltpu.roll(gridded, SUBG, 1)
    turned = jnp.where(half, turned, -turned)
    gridded = jnp.concatenate([gridded, turned], 0).astype(BF16)
    parts = dot(row_wide[...], gridded)
    image_send[...] = parts.astype(BF16).reshape(facet_count, sub_count, rows, LANES)
    send_all(3, across, lambda f, s: image_send.at[f], image_stage.at[my_facet])
    send_all(
        2, partners, lambda f, s: back_send.at[lax.div(f * sub_count + s, group)], back_recv.at[me]
    )
    image_stage[my_facet] = image_send[my_facet]
    back_recv[me] = back_send[lax.div(me, group)]

    wait_all(recv_sems, 3, image_stage)
    images = image_stage[0].astype(F32)
    for f in range(1, facet_count):
        images = images + image_stage[f].astype(F32)
    image_sum[...] = images.astype(BF16)
    send_all(5, beside, lambda f, s: image_sum.at[s], image_recv.at[my_sub])
    image_recv[my_sub] = image_sum[my_sub]

    wait_all(recv_sems, 2, back_recv)
    returned = back_recv[...].reshape(devices * 2, LANES)
    parts = dot(jnp.concatenate(three_parts(returned), 0), place_ref[...])
    count = devices * 2
    found = parts[:count] + parts[count : 2 * count] + parts[2 * count :]
    row = iota((devices * 2, vis), 0).astype(F32)
    wanted = owner_ref[...] * 2.0
    residual_ref[0:1, :] = jnp.sum(jnp.where(row == wanted, found, 0.0), 0, keepdims=True)
    residual_ref[1:2, :] = jnp.sum(jnp.where(row == wanted + 1.0, found, 0.0), 0, keepdims=True)

    wait_all(recv_sems, 5, image_recv)
    image_ref[...] = image_recv[...].astype(F32).reshape(columns * rows, LANES)

    wait_all(send_sems, 0, vis_recv)
    wait_all(send_sems, 1, spec_stage)
    wait_all(send_sems, 2, back_recv)
    wait_all(send_sems, 3, image_stage)
    wait_all(send_sems, 4, spec_recv)
    wait_all(send_sems, 5, image_recv)
    wait_all(send_sems, 6, start_recv)


def adjoint_kernel(
    columns,
    width,
    offsets_ref,
    image_ref,
    found_ref,
    adjoint_ref,
    residual_ref,
    matrix,
    step_cos,
    step_sin,
    straight,
    crossed,
    image_held,
    sems,
):
    rows = adjoint_ref.shape[2]
    block_steps = adjoint_ref.shape[3] // LANES

    @pl.when(pl.program_id(0) == 0)
    def first():
        image_copy = pltpu.make_async_copy(image_ref, image_held, sems.at[0])
        found_copy = pltpu.make_async_copy(found_ref, residual_ref, sems.at[1])
        image_copy.start()
        found_copy.start()
        column_tables(offsets_ref[0, 1], columns, width, matrix, step_cos, step_sin)
        image_copy.wait()
        found_copy.wait()
        for q in range(columns):
            image = image_held[q * rows : (q + 1) * rows, :]
            at = slice(q * LANES, (q + 1) * LANES)
            straight[:, at] = image
            crossed[:, at] = pltpu.roll(image, SUBG, 1)

    start = pl.program_id(0) * block_steps
    pieces = []
    for h in range(block_steps):
        sc = step_cos[pl.ds(start + h, 1), :]
        ss = step_sin[pl.ds(start + h, 1), :]
        piece = []
        for q in range(columns):
            at = slice(q * LANES, (q + 1) * LANES)
            piece.append((straight[:, at] * sc + crossed[:, at] * ss).astype(BF16))
        pieces.append(jnp.concatenate(piece, 1))
    out = dot_nt(jnp.concatenate(pieces, 0), matrix[...])
    for h in range(block_steps):
        at = slice(h * LANES, (h + 1) * LANES)
        adjoint_ref[0, 0, :, at] = out[h * rows : (h + 1) * rows, :LANES]
        adjoint_ref[0, 1, :, at] = out[h * rows : (h + 1) * rows, LANES:]


def on_device(
    facet_slab, facet_offsets, visibility_position, observed, visibility_subgrid, clip_levels
):
    sub_count = lax.axis_size("sub")
    facet_count = lax.axis_size("facet")
    devices = sub_count * facet_count
    rows = facet_slab.shape[2]
    width = facet_slab.shape[3]
    vis = visibility_position.shape[1]
    most = max(2, 2 * vis // (PR_DEV * facet_count * sub_count))
    slots = devices * PR_DEV * most
    all_rows = devices * rows
    vmem = pl.BlockSpec(memory_space=pltpu.VMEM)
    smem = pl.BlockSpec(memory_space=pltpu.SMEM)
    images, found = pl.pallas_call(
        functools.partial(kernel, facet_count, sub_count),
        out_shape=(
            jax.ShapeDtypeStruct((sub_count * rows, LANES), F32),
            jax.ShapeDtypeStruct((2, vis), F32),
        ),
        in_specs=[smem] + [vmem] * 5,
        out_specs=(vmem, vmem),
        scratch_shapes=[
            pltpu.VMEM((8, LANES), F32),
            pltpu.VMEM((facet_count, 8, LANES), F32),
            pltpu.VMEM((devices, 8, LANES), F32),
            pltpu.VMEM((devices, 8, LANES), F32),
            pltpu.VMEM((sub_count, rows, LANES), BF16),
            pltpu.VMEM((sub_count, rows, LANES), BF16),
            pltpu.VMEM((facet_count, sub_count, rows, LANES), BF16),
            pltpu.VMEM((slots // LANES, 2, LANES), F32),
            pltpu.VMEM((devices, 2, LANES), F32),
            pltpu.VMEM((facet_count, sub_count, rows, LANES), BF16),
            pltpu.VMEM((facet_count, sub_count, rows, LANES), BF16),
            pltpu.VMEM((sub_count, rows, LANES), BF16),
            pltpu.VMEM((sub_count, rows, LANES), BF16),
            pltpu.VMEM((LANES, vis), BF16),
            pltpu.VMEM((1, vis), F32),
            pltpu.VMEM((width // LANES * rows, 2 * LANES), BF16),
            pltpu.VMEM((2 * LANES, sub_count * LANES), BF16),
            pltpu.VMEM((width // LANES, LANES), F32),
            pltpu.VMEM((width // LANES, LANES), F32),
            pltpu.VMEM((all_rows, 2 * LANES), BF16),
            pltpu.VMEM((2 * LANES, all_rows), BF16),
            pltpu.VMEM((SUBG, slots), F32),
            pltpu.VMEM((SUBG, slots), F32),
            pltpu.VMEM((2 * SUBG, slots), BF16),
            pltpu.VMEM((2 * SUBG, slots), BF16),
            pltpu.VMEM((8, slots), F32),
            pltpu.SemaphoreType.DMA((7,)),
            pltpu.SemaphoreType.DMA((7,)),
        ],
        compiler_params=pltpu.CompilerParams(
            collective_id=0, has_side_effects=True, vmem_limit_bytes=56 * 1024 * 1024
        ),
    )(
        facet_offsets,
        facet_slab,
        visibility_position,
        observed,
        visibility_subgrid.reshape(1, vis),
        clip_levels.reshape(1, -1),
    )
    blocks = 4
    whole = lambda *shape: pl.BlockSpec(shape, lambda i: (0,) * len(shape))
    return pl.pallas_call(
        functools.partial(adjoint_kernel, sub_count, width),
        grid=(blocks,),
        out_shape=(
            jax.ShapeDtypeStruct(facet_slab.shape, F32),
            jax.ShapeDtypeStruct((2, vis), F32),
        ),
        in_specs=[smem] + [pl.BlockSpec(memory_space=pl.ANY)] * 2,
        out_specs=(
            pl.BlockSpec((1, 2, rows, width // blocks), lambda i: (0, 0, 0, i)),
            whole(2, vis),
        ),
        scratch_shapes=[
            pltpu.VMEM((2 * LANES, sub_count * LANES), BF16),
            pltpu.VMEM((width // LANES, LANES), F32),
            pltpu.VMEM((width // LANES, LANES), F32),
            pltpu.VMEM((rows, sub_count * LANES), F32),
            pltpu.VMEM((rows, sub_count * LANES), F32),
            pltpu.VMEM((sub_count * rows, LANES), F32),
            pltpu.SemaphoreType.DMA((2,)),
        ],
        compiler_params=pltpu.CompilerParams(vmem_limit_bytes=60 * 1024 * 1024),
    )(facet_offsets, images, found)


def solution(mesh):
    placed = (
        P("facet", None, "sub", None),
        P("facet", None),
        P(None, ("facet", "sub")),
        P(None, ("facet", "sub")),
        P(("facet", "sub"), None),
        P(("facet", "sub")),
    )
    return jax.shard_map(
        on_device,
        mesh=mesh,
        in_specs=placed,
        out_specs=(P("facet", None, "sub", None), P(None, ("facet", "sub"))),
        check_vma=False,
    )
```
